128 devices in a mesh: section: 2 (over x_lo), dp: 4 (over x_hi, core), mp: 16 (over y, z).
Axes of the slice: x: 4 (x_hi: 2, x_lo: 2; x = x_hi * 2 + x_lo), y: 4, z: 4, core: 2. Of those that a mesh axis runs over, the one named last changes fastest.
Arguments:
- late_inputs: bfloat16 [1024, 8192], P('dp'), may hold values from -6 to 6
- cotangent: bfloat16 [1024, 8192], P('dp'), may hold values from -6 to 6
- early_inputs: bfloat16 [1024, 8192], P('dp'), may hold values from -6 to 6
- doc_lengths: int32 [4, 4], P('dp'), may hold values from 1 to 128, 256 in all within a row
- norm_gain: bfloat16 [2, 8192], P('section'), may hold values from 0.5 to 1.5
- w_query: bfloat16 [2, 8192, 4096], P('section', None, 'mp'), may hold values from -0.0625 to 0.0625
- w_key: bfloat16 [2, 8192, 512], P('section', None, 'mp'), may hold values from -0.0625 to 0.0625
- w_value: bfloat16 [2, 8192, 512], P('section', None, 'mp'), may hold values from -0.0625 to 0.0625
- w_output: bfloat16 [2, 8192, 4096], P('section', None, 'mp'), may hold values from -0.09375 to 0.09375
Outputs:
- input_grads: bfloat16 [2, 1024, 8192], P('section', 'dp', 'mp')
- grad_query: bfloat16 [2, 8192, 4096], P('section', 'dp', 'mp')
- grad_key: bfloat16 [2, 8192, 512], P('section', 'dp', 'mp')
- grad_value: bfloat16 [2, 8192, 512], P('section', 'dp', 'mp')
- grad_output: bfloat16 [2, 8192, 4096], P('section', 'dp', 'mp')
The draws below stay inside these ranges and needn't reach their ends.
Inputs may be any that keep to these rules, and one draw needn't show every extreme that they name: `doc_lengths`: each row lists the lengths of 4 documents that fill one sequence of 256 tokens.
All inputs are finite; a program needn't handle non-finite values.
Results may differ from the reference program's by a relative error of at most 0.028.
Values may be sent and summed in bfloat16 or wider, within the bound.
A program may use at most 192 MiB of HBM per device.

```python
import math
import jax
import jax.numpy as jnp
import numpy as np
from jax import lax

D = 8192
HD = 128
HEADS = 32
KVH = 4
SEQ = 256
NDOC = 4
SEQS = 4
TOK = 1024
N_MP = 16


def levels(rng, extent, cuts, smallest, largest):
    level = 1.0
    for position, parts in cuts:
        steps = jax.random.uniform(jax.random.fold_in(jax.random.fold_in(rng, 6), position), (parts,), jnp.float32, smallest / len(cuts), largest / len(cuts))
        level = level * jnp.repeat(jnp.exp(steps), extent[position] // parts).reshape((-1,) + (1,) * (len(extent) - 1 - position))
    return level


def split_up(count, total, bound, lean):
    loads = [(1 << 20) // math.isqrt(grade ** lean) + 1 for grade in range(2, count + 1)]
    surplus, holding = total - bound - (count - 1), [1] * (count - 1)
    while surplus > 0:
        movable = [i for i in range(count - 1) if holding[i] < bound]
        mass, left = sum([loads[i] for i in movable]), surplus
        for i in movable:
            addition = min(bound - holding[i], max(1, left * loads[i] // mass), surplus)
            holding[i] = holding[i] + addition
            surplus = surplus - addition
    return np.array([bound] + holding)


def ragged(own_key, number_of, total, bound, skew):
    if number_of == 2:
        one = jax.random.randint(own_key, (), max(1, total - bound), min(bound, total - 1) + 1)
        return jnp.stack([one, total - one])
    sizes = jnp.asarray(split_up(number_of, total, bound, skew), jnp.int32)
    twos = (number_of - 1) // 2
    source_of, receiver = sizes[1:1 + 2 * twos:2], sizes[2:2 + 2 * twos:2]
    room = jnp.minimum(source_of - 1, bound - receiver)
    passed = jax.random.randint(jax.random.fold_in(own_key, 1), (twos,), 0, 1 << 20) % (room + 1)
    sizes = sizes.at[1:1 + 2 * twos:2].set(source_of - passed).at[2:2 + 2 * twos:2].set(receiver + passed)
    return sizes[jax.random.permutation(jax.random.fold_in(own_key, 2), number_of)]


def noise(rng, dims, scale, bound, cuts=(), kind=jnp.bfloat16):
    array = scale * jax.random.normal(rng, dims, jnp.float32)
    if cuts:
        array = array * levels(rng, dims, cuts, -0.22, 0.18)
    return jnp.clip(array, -bound, bound).astype(kind)


def setup_inputs(seed: int = 0) -> dict:
    streams_of = jax.random.split(jax.random.key(seed), 10)
    late_inputs = noise(streams_of[0], (TOK, D), 1.0, 6.0, ((0, 4),))
    cotangent = noise(streams_of[1], (TOK, D), 1.0, 6.0, ((0, 4),))
    early_inputs = noise(streams_of[2], (TOK, D), 1.0, 6.0, ((0, 4),))
    doc_lengths = jax.vmap(lambda own: ragged(own, NDOC, SEQ, SEQ // 2, 2))(jax.random.split(streams_of[3], SEQS)).reshape((SEQS, NDOC)).astype(jnp.int32)
    norm_gain = jnp.clip(1.0 + 0.1 * jax.random.normal(streams_of[4], (2, D), jnp.float32), 0.5, 1.5).astype(jnp.bfloat16)
    w_query = noise(streams_of[5], (2, D, HEADS * HD), D ** -0.5, 0.0625, ((0, 2), (2, 16)))
    w_key = noise(streams_of[6], (2, D, KVH * HD), D ** -0.5, 0.0625, ((0, 2), (2, 16)))
    w_value = noise(streams_of[7], (2, D, KVH * HD), D ** -0.5, 0.0625, ((0, 2), (2, 16)))
    w_output = noise(streams_of[8], (2, D, HEADS * HD), (HEADS * HD) ** -0.5, 0.09375, ((0, 2), (2, 16)))
    return dict(late_inputs=late_inputs, cotangent=cotangent, early_inputs=early_inputs, doc_lengths=doc_lengths, norm_gain=norm_gain, w_query=w_query, w_key=w_key, w_value=w_value, w_output=w_output)


def doc_tables(lengths, seq_len, head_size):
    starts = (jnp.cumsum(lengths) - lengths).astype(jnp.int32)
    places = jnp.arange(seq_len, dtype=jnp.int32)
    begins = lax.optimization_barrier(jnp.max(jnp.where(starts[None, :] <= places[:, None], starts[None, :], jnp.zeros_like(starts)[None, :]), axis=1)).astype(jnp.int32)
    offsets = (places - begins).astype(jnp.float32)
    frequencies = 10000.0 ** (-jnp.arange(0, head_size, 2).astype(jnp.float32) / head_size)
    angles = offsets[:, None] * frequencies[None, :]
    cosine = jnp.concatenate([jnp.cos(angles), jnp.cos(angles)], axis=1)
    sine_table = jnp.concatenate([jnp.sin(angles), jnp.sin(angles)], axis=1)
    allowed = (begins[:, None] == begins[None, :]) & (places[None, :] <= places[:, None])
    return (cosine, sine_table, allowed)

def rotate(values):
    half_size = values.shape[-1] // 2
    return jnp.concatenate([-values[..., half_size:], values[..., :half_size]], axis=-1)

def apply_rope(values, cosine, sine_table):
    return values * cosine + rotate(values) * sine_table

def undo_rope(values, cosine, sine_table):
    return values * cosine - rotate(values * sine_table)

def batch_mix(pattern, first_op, second_op):
    return jnp.einsum(pattern, first_op.astype(jnp.float32), second_op.astype(jnp.float32))

def matmul_nt(first_op, second_op):
    return lax.dot_general(first_op, second_op, (((1,), (1,)), ((), ())), preferred_element_type=jnp.float32)

def matmul_tn(first_op, second_op):
    return lax.dot_general(first_op, second_op, (((0,), (0,)), ((), ())), preferred_element_type=jnp.float32)

def head_block(tokens, upstream, norm_weight, w_query, w_key, w_value, w_output, cosine, sine_table, allowed):
    seq_len = tokens.shape[0]
    head_size = cosine.shape[1]
    query_heads = w_query.shape[1] // head_size
    key_heads = w_key.shape[1] // head_size
    repeats = query_heads // key_heads
    score_scale = 1.0 / math.sqrt(head_size)
    cos_rows = cosine[:, None, :]
    sin_rows = sine_table[:, None, :]
    token_f32 = tokens.astype(jnp.float32)
    gain_f32 = norm_weight.astype(jnp.float32)
    inv_rms = lax.rsqrt(lax.optimization_barrier(jnp.mean(token_f32 * token_f32, axis=1)) + 1e-05)
    normed = (token_f32 * inv_rms[:, None] * gain_f32).astype(jnp.bfloat16)
    queries = apply_rope(jnp.dot(normed, w_query, preferred_element_type=jnp.float32).reshape(seq_len, query_heads, head_size), cos_rows, sin_rows).astype(jnp.bfloat16)
    key_rows = apply_rope(jnp.dot(normed, w_key, preferred_element_type=jnp.float32).reshape(seq_len, key_heads, head_size), cos_rows, sin_rows).astype(jnp.bfloat16)
    value_rows = jnp.dot(normed, w_value, preferred_element_type=jnp.float32).astype(jnp.bfloat16).reshape(seq_len, key_heads, head_size)
    key_wide = jnp.repeat(key_rows, repeats, axis=1)
    value_wide = jnp.repeat(value_rows, repeats, axis=1)
    scores = batch_mix('thd,shd->hts', queries, key_wide) * score_scale
    scores = jnp.where(allowed[None, :, :], scores, -1e+30)
    row_peak = lax.optimization_barrier(jnp.max(scores, axis=2, keepdims=True))
    exp_scores = jnp.exp(scores - row_peak)
    probs = exp_scores / lax.optimization_barrier(jnp.sum(exp_scores, axis=2, keepdims=True))
    probs_low = probs.astype(jnp.bfloat16)
    context = batch_mix('hts,shd->thd', probs_low, value_wide).astype(jnp.bfloat16)
    grad_context = jnp.dot(upstream, w_output, preferred_element_type=jnp.float32).astype(jnp.bfloat16).reshape(seq_len, query_heads, head_size)
    grad_probs = batch_mix('thd,shd->hts', grad_context, value_wide)
    grad_scores = (probs * (grad_probs - lax.optimization_barrier(jnp.sum(grad_probs * probs, axis=2, keepdims=True))) * score_scale).astype(jnp.bfloat16)
    grad_queries = undo_rope(batch_mix('hts,shd->thd', grad_scores, key_wide), cos_rows, sin_rows).astype(jnp.bfloat16)
    key_sum = batch_mix('hts,thd->shd', grad_scores, queries).reshape(seq_len, key_heads, repeats, head_size).sum(axis=2)
    key_part = undo_rope(key_sum, cos_rows, sin_rows).astype(jnp.bfloat16)
    value_part = batch_mix('hts,thd->shd', probs_low, grad_context).reshape(seq_len, key_heads, repeats, head_size).sum(axis=2).astype(jnp.bfloat16)
    flat_query = grad_queries.reshape(seq_len, query_heads * head_size)
    flat_key = key_part.reshape(seq_len, key_heads * head_size)
    flat_value = value_part.reshape(seq_len, key_heads * head_size)
    grad_normed = matmul_nt(flat_query, w_query) + matmul_nt(flat_key, w_key) + matmul_nt(flat_value, w_value)
    stat_part = lax.optimization_barrier(jnp.sum(token_f32 * gain_f32 * grad_normed, axis=1))
    return (grad_normed, stat_part, flat_key, flat_value, flat_query, context.reshape(seq_len, query_heads * head_size), normed, inv_rms)

def layer_backward(tokens, upstream, lengths, norm_weight, w_query, w_key, w_value, w_output):
    seq_count = lengths.shape[0]
    seq_len = tokens.shape[0] // seq_count
    width = tokens.shape[1]
    tok_seq = tokens.reshape(seq_count, seq_len, width)
    up_seq = upstream.reshape(seq_count, seq_len, width)
    cosine, sine_table, allowed = jax.vmap(doc_tables, in_axes=(0, None, None))(lengths, seq_len, HD)
    heads_group = HEADS // N_MP
    query_cols = heads_group * HD
    group_size = HEADS // KVH
    kv_group = max(1, heads_group // group_size)
    mapped = jax.vmap(head_block, in_axes=(0, 0, None, None, None, None, None, 0, 0, 0))
    grad_normed = jnp.zeros((seq_count, seq_len, width), jnp.float32)
    stat_total = jnp.zeros((seq_count, seq_len), jnp.float32)
    key_total = jnp.zeros((seq_count, seq_len, KVH * HD), jnp.float32)
    value_total = jnp.zeros((seq_count, seq_len, KVH * HD), jnp.float32)
    query_list = []
    context_list = []
    normed = None
    inv_rms = None
    for group_index in range(N_MP):
        key_first = group_index * heads_group // group_size * HD
        key_last = key_first + kv_group * HD
        query_first = group_index * query_cols
        pieces = mapped(tok_seq, up_seq, norm_weight, w_query[:, query_first:query_first + query_cols], w_key[:, key_first:key_last], w_value[:, key_first:key_last], w_output[:, query_first:query_first + query_cols], cosine, sine_table, allowed)
        grad_normed = grad_normed + pieces[0]
        stat_total = stat_total + pieces[1]
        key_total = key_total.at[:, :, key_first:key_last].add(pieces[2].astype(jnp.float32))
        value_total = value_total.at[:, :, key_first:key_last].add(pieces[3].astype(jnp.float32))
        query_list.append(pieces[4])
        context_list.append(pieces[5])
        normed = pieces[6]
        inv_rms = pieces[7]
    grad_keys = key_total.astype(jnp.bfloat16)
    grad_values = value_total.astype(jnp.bfloat16)
    grad_queries = jnp.concatenate(query_list, axis=2)
    contexts = jnp.concatenate(context_list, axis=2)
    token_f32 = tok_seq.astype(jnp.float32)
    gain_f32 = norm_weight.astype(jnp.float32)
    grad_in = (up_seq.astype(jnp.float32) + inv_rms[..., None] * gain_f32 * grad_normed - token_f32 * (inv_rms ** 3 * stat_total / width)[..., None]).astype(jnp.bfloat16)
    total_rows = seq_count * seq_len
    normed_flat = normed.reshape(total_rows, width)
    grad_query = matmul_tn(normed_flat, grad_queries.reshape(total_rows, HEADS * HD))
    grad_key = matmul_tn(normed_flat, grad_keys.reshape(total_rows, KVH * HD))
    grad_value = matmul_tn(normed_flat, grad_values.reshape(total_rows, KVH * HD))
    grad_output = matmul_tn(upstream, contexts.reshape(total_rows, HEADS * HD))
    return (grad_in.reshape(total_rows, width), grad_query, grad_key, grad_value, grad_output)

def reference(late_inputs, cotangent, early_inputs, doc_lengths, norm_gain, w_query, w_key, w_value, w_output):
    later = layer_backward(late_inputs, cotangent, doc_lengths, norm_gain[1], w_query[1], w_key[1], w_value[1], w_output[1])
    earlier = layer_backward(early_inputs, later[0], doc_lengths, norm_gain[0], w_query[0], w_key[0], w_value[0], w_output[0])
    input_grads = jnp.stack([earlier[0], later[0]])
    grad_query = jnp.stack([earlier[1], later[1]]).astype(jnp.bfloat16)
    grad_key = jnp.stack([earlier[2], later[2]]).astype(jnp.bfloat16)
    grad_value = jnp.stack([earlier[3], later[3]]).astype(jnp.bfloat16)
    grad_output = jnp.stack([earlier[4], later[4]]).astype(jnp.bfloat16)
    return (input_grads, grad_query, grad_key, grad_value, grad_output)
```

```python
import functools
import math

import jax
import jax.numpy as jnp
import numpy as np
from jax import lax
from jax.experimental import pallas as pl
from jax.experimental.pallas import tpu as pltpu
from jax.sharding import PartitionSpec as P

HD = 128
SEQ = 256
D = 8192
TILE = 512
BLOCK = 2048
KV = 64
ROWS = 320
CHUNK = 1024
N_CHUNK = D // CHUNK
SCALE = 1.0 / math.sqrt(HD)
F32 = jnp.float32
BF16 = jnp.bfloat16
MESH = pl.DeviceIdType.MESH


def dot_nn(a, b):
    return lax.dot_general(a, b, (((1,), (0,)), ((), ())), preferred_element_type=F32)


def dot_nt(a, b):
    return lax.dot_general(a, b, (((1,), (1,)), ((), ())), preferred_element_type=F32)


def ring(v):
    return lax.rem(v + 4, 4)


def begin_of(lens, places):
    start = jnp.int32(0)
    begins = jnp.zeros_like(places)
    for i in range(4):
        begins = jnp.maximum(begins, jnp.where(places >= start, start, 0))
        start = start + lens[0, i]
    return begins


def swap_rows(v):
    return jnp.concatenate([v[64:128], v[0:64]], axis=0)


def relay_kernel(
    late, cot, early, lens, gain, w_q, w_k, w_v, w_o, freq,
    gin, tok_g, up_g, d_g, c_g,
    tok, wq, wkv, wo, up, part,
    xq, xkv, dctx, probs, qs, kv_all, kvp_send, kvp_recv, cosv, sinv, inv_ref, cs_ref,
    aq, akv, dqkv, ctx,
    rrel, racc, rdir, summed, rrel2, racc2, rdir2,
    load_sem, up_sem, loc_sem, send_sem, recv_sem,
):
    s = lax.axis_index("section")
    d = lax.axis_index("dp")
    m = lax.axis_index("mp")
    y, z = lax.div(m, 4), lax.rem(m, 4)
    h, c = lax.div(d, 2), lax.rem(d, 2)
    d_of = [d, h * 2 + (1 - c), (1 - h) * 2 + c, (1 - h) * 2 + (1 - c)]
    is_later = s == 1
    is_earlier = s == 0

    def mp_id(yy, zz):
        return {"mp": yy * 4 + zz}

    z_peer = [mp_id(y, ring(z + o)) for o in range(4)]
    y_right, y_left = mp_id(ring(y + 1), z), mp_id(ring(y - 1), z)
    z_right, z_left = z_peer[1], z_peer[3]
    dp_peer = [{"dp": d_of[o]} for o in range(4)]
    cross_peer = [None, None] + [{"section": 1 - s, "dp": d_of[o]} for o in (2, 3)]
    hand_peer = {"section": 1 - s}

    def tok_copy(source, i):
        return pltpu.make_async_copy(
            source.at[:, pl.ds(i * CHUNK, CHUNK)], tok.at[:, pl.ds(i * CHUNK, CHUNK)], load_sem.at[0, i]
        )

    def wq_copy(i):
        return pltpu.make_async_copy(
            w_q.at[pl.ds(i * CHUNK, CHUNK), :], wq.at[pl.ds(i * CHUNK, CHUNK), :], load_sem.at[1, i]
        )

    def wk_copy(i):
        return pltpu.make_async_copy(
            w_k.at[:, pl.ds(i * CHUNK, CHUNK)], wkv.at[0:32, pl.ds(i * CHUNK, CHUNK)], load_sem.at[2, i]
        )

    def wv_copy(i):
        return pltpu.make_async_copy(
            w_v.at[:, pl.ds(i * CHUNK, CHUNK)], wkv.at[32:64, pl.ds(i * CHUNK, CHUNK)], load_sem.at[3, i]
        )

    def wo_copy(i):
        return pltpu.make_async_copy(
            w_o.at[pl.ds(i * CHUNK, CHUNK), :], wo.at[pl.ds(i * CHUNK, CHUNK), :], load_sem.at[4, i]
        )

    def cot_copy(yy, zz):
        return pltpu.make_async_copy(
            cot.at[:, pl.ds(pl.multiple_of((yy * 4 + zz) * TILE, TILE), TILE)], up.at[yy, zz], up_sem.at[yy, zz]
        )

    def per_section(later, earlier):
        pl.when(is_later)(later)
        pl.when(is_earlier)(earlier)

    for i in range(N_CHUNK):
        per_section(lambda: tok_copy(late, i).start(), lambda: tok_copy(early, i).start())
        wq_copy(i).start()
        wk_copy(i).start()
        wv_copy(i).start()
    for i in range(N_CHUNK):
        wo_copy(i).start()

    @pl.when(is_later)
    def _():
        for yy in range(4):
            for zz in range(4):
                cot_copy(yy, zz).start()

    barrier = pltpu.get_barrier_semaphore()
    greeted = [z_peer[1], z_peer[2], z_peer[3], y_right, y_left, hand_peer]
    greeted += dp_peer[1:] + cross_peer[2:]
    for peer in greeted:
        pl.semaphore_signal(barrier, inc=1, device_id=peer, device_id_type=MESH)
    pl.semaphore_wait(barrier, len(greeted))

    count = [0]

    def slot():
        count[0] += 1
        return count[0] - 1

    def remote(src, dst, n, peer):
        return pltpu.make_async_remote_copy(
            src_ref=src, dst_ref=dst, send_sem=send_sem.at[n], recv_sem=recv_sem.at[n],
            device_id=peer, device_id_type=MESH,
        )

    def cols(index):
        return pl.ds(pl.multiple_of(index * BLOCK, BLOCK), BLOCK)

    tok_slots = [None] + [slot() for _ in range(3)]
    up_slots = [None] + [slot() for _ in range(3)]

    def tok_send(source, o):
        peer = dp_peer[1] if o == 1 else cross_peer[o]
        return remote(source.at[:, cols(d_of[o])], tok_g.at[d], tok_slots[o], peer)

    def cot_send(o):
        peer = dp_peer[1] if o == 1 else cross_peer[o]
        return remote(cot.at[:, cols(d_of[o])], up_g.at[d], up_slots[o], peer)

    def tok_keep(source):
        return pltpu.make_async_copy(source.at[:, cols(d)], tok_g.at[d], loc_sem.at[0])

    def cot_keep():
        return pltpu.make_async_copy(cot.at[:, cols(d)], up_g.at[d], loc_sem.at[1])

    def later_starts():
        tok_send(late, 1).start()
        tok_send(early, 2).start()
        tok_send(early, 3).start()
        cot_send(1).start()
        tok_keep(late).start()
        cot_keep().start()

    def earlier_starts():
        tok_send(early, 1).start()
        tok_send(late, 2).start()
        tok_send(late, 3).start()
        cot_send(2).start()
        cot_send(3).start()
        tok_keep(early).start()

    per_section(later_starts, earlier_starts)

    lane = lax.broadcasted_iota(jnp.int32, (SEQ, HD), 1)
    place = lax.broadcasted_iota(jnp.int32, (SEQ, HD), 0)
    offset = (place - begin_of(lens, place)).astype(F32)
    angle = offset * freq[0:1, :]
    cosv[...] = jnp.cos(angle)
    sinv[...] = jnp.where(lane < 64, -1.0, 1.0) * jnp.sin(angle)

    xq[...] = jnp.zeros_like(xq)
    xkv[...] = jnp.zeros_like(xkv)
    inv_ref[...] = jnp.zeros_like(inv_ref)

    def project(i, carry):
        span = pl.ds(pl.multiple_of(i * CHUNK, CHUNK), CHUNK)
        tok_copy(late, i).wait()
        wq_copy(i).wait()
        wk_copy(i).wait()
        wv_copy(i).wait()
        t = tok[:, span].astype(F32)
        x = (t * gain[0:1, span].astype(F32)).astype(BF16)
        inv_ref[...] += jnp.sum(t * t, axis=1, keepdims=True)
        xq[...] += dot_nn(x, wq[span, :])
        xkv[...] += dot_nt(x, wkv[:, span])
        return carry

    lax.fori_loop(0, N_CHUNK, project, 0)
    inv_ref[...] = lax.rsqrt(inv_ref[...] * (1.0 / D) + 1e-5)
    inv = inv_ref[:, 0:1]

    kv_all[z] = jnp.transpose(xkv[...] * inv).astype(BF16)
    kv_slots = [None] + [slot() for _ in range(3)]
    kv_copies = [remote(kv_all.at[z], kv_all.at[z], kv_slots[o], z_peer[o]) for o in (1, 2, 3)]
    for copy in kv_copies:
        copy.start()

    cos = cosv[...]
    sin = sinv[...]
    cos_t = jnp.transpose(cos)
    sin_t = jnp.transpose(sin)
    for j in range(2):
        q = xq[:, j * HD:(j + 1) * HD] * inv
        qs[j] = (q * cos + pltpu.roll(q, 64, 1) * sin).astype(BF16)
    for copy in kv_copies:
        copy.wait_recv()
    k = jnp.concatenate([kv_all[i, 0:32] for i in range(4)], axis=0).astype(F32)
    k_t = (k * cos_t + swap_rows(k) * sin_t).astype(BF16)
    v_t = jnp.concatenate([kv_all[i, 32:64] for i in range(4)], axis=0)

    row = lax.broadcasted_iota(jnp.int32, (SEQ, SEQ), 0)
    col = lax.broadcasted_iota(jnp.int32, (SEQ, SEQ), 1)
    allowed = (begin_of(lens, row) == begin_of(lens, col)) & (col <= row)
    for j in range(2):
        scores = jnp.where(allowed, dot_nn(qs[j], k_t) * SCALE, -1e30)
        peak = jnp.max(scores, axis=1, keepdims=True)
        ex = jnp.exp(scores - peak)
        pr = ex / jnp.sum(ex, axis=1, keepdims=True)
        probs[j] = pr
        ctx[j * HD:(j + 1) * HD, :] = dot_nt(v_t, pr.astype(BF16)).astype(BF16)
    ctx_slots = [None] + [slot() for _ in range(3)]
    ctx_copies = [remote(ctx, c_g.at[d], ctx_slots[o], dp_peer[o]) for o in (1, 2, 3)]
    ctx_keep = pltpu.make_async_copy(ctx, c_g.at[d], loc_sem.at[2])
    for copy in ctx_copies:
        copy.start()
    ctx_keep.start()

    for i in range(N_CHUNK):
        wo_copy(i).wait()
    dctx[...] = jnp.zeros_like(dctx)

    def wo_rows(yy, zz):
        return pl.ds(pl.multiple_of((yy * 4 + zz) * TILE, TILE), TILE)

    def halves(k):
        return pl.ds(k * 128, 128)

    def add_context(k, yy, zz):
        dctx[halves(k), :] += dot_nn(up[yy, zz, halves(k), :], wo[wo_rows(yy, zz), :])

    own_slots = [slot() for _ in range(2)]
    p1_slots = [[slot() for _ in range(4)] for _ in range(2)]
    p2_slots = [[[slot() for _ in range(4)] for _ in range(4)] for _ in range(2)]

    def hand_copy(k):
        return remote(up.at[y, z, halves(k), :], up.at[y, z, halves(k), :], own_slots[k], hand_peer)

    def at(k, first, second):
        return (second, first) if k == 0 else (first, second)

    @pl.when(is_later)
    def _():
        def body(i, carry):
            yy, zz = lax.div(i, 4), lax.rem(i, 4)
            cot_copy(yy, zz).wait()
            dctx[...] += dot_nn(up[yy, zz], wo[wo_rows(yy, zz), :])
            return carry

        lax.fori_loop(0, 16, body, 0)

    @pl.when(is_earlier)
    def _():
        first_of, second_of = (z, y), (y, z)
        first_right, first_left = (z_right, y_right), (z_left, y_left)
        second_right, second_left = (y_right, z_right), (y_left, z_left)
        pending = []

        def piece(k, a, b, lo, n):
            yy, zz = at(k, a, b)
            return up.at[yy, zz, pl.ds(k * 128 + lo, n), :]

        def send(k, a, b, lo, n, index, peer):
            ref = piece(k, a, b, lo, n)
            copy = remote(ref, ref, index, peer)
            copy.start()
            pending.append(copy)

        def arrived(k, a, b, lo, n, index):
            ref = piece(k, a, b, lo, n)
            remote(ref, ref, index, hand_peer).wait_recv()

        def spread(k, o):
            a = ring(first_of[k] + o)
            send(k, a, second_of[k], 0, 128, p2_slots[k][o][0], second_right[k])
            send(k, a, second_of[k], 0, 128, p2_slots[k][o][1], second_left[k])

        for k in range(2):
            hand_copy(k).wait_recv()
            send(k, first_of[k], second_of[k], 0, 128, p1_slots[k][0], first_right[k])
            send(k, first_of[k], second_of[k], 0, 128, p1_slots[k][1], first_left[k])
            spread(k, 0)
        for k in range(2):
            add_context(k, y, z)
        for k in range(2):
            a, b = ring(first_of[k] - 1), second_of[k]
            arrived(k, a, b, 0, 128, p1_slots[k][0])
            send(k, a, b, 0, 64, p1_slots[k][2], first_right[k])
            spread(k, 3)
            a = ring(first_of[k] + 1)
            arrived(k, a, b, 0, 128, p1_slots[k][1])
            send(k, a, b, 64, 64, p1_slots[k][3], first_left[k])
            spread(k, 1)
        for k in range(2):
            for o in (3, 1):
                add_context(k, *at(k, ring(first_of[k] + o), second_of[k]))

        def relay(k, o):
            a = ring(first_of[k] + o)
            left, right = ring(second_of[k] - 1), ring(second_of[k] + 1)
            arrived(k, a, left, 0, 128, p2_slots[k][o][0])
            send(k, a, left, 0, 64, p2_slots[k][o][2], second_right[k])
            arrived(k, a, right, 0, 128, p2_slots[k][o][1])
            send(k, a, right, 64, 64, p2_slots[k][o][3], second_left[k])
            add_context(k, *at(k, a, left))
            add_context(k, *at(k, a, right))

        for k in range(2):
            relay(k, 0)
        for k in range(2):
            a, b = ring(first_of[k] + 2), second_of[k]
            arrived(k, a, b, 0, 64, p1_slots[k][2])
            arrived(k, a, b, 64, 64, p1_slots[k][3])
            spread(k, 2)
            add_context(k, *at(k, a, b))
        for o in (3, 1, 2):
            for k in range(2):
                relay(k, o)
        for o in (0, 3, 1, 2):
            for k in range(2):
                a, b = ring(first_of[k] + o), ring(second_of[k] + 2)
                arrived(k, a, b, 0, 64, p2_slots[k][o][2])
                arrived(k, a, b, 64, 64, p2_slots[k][o][3])
                add_context(k, *at(k, a, b))
        for copy in pending:
            copy.wait_send()
        for o in (2, 3, 1):
            for zz in range(4):
                remote(
                    up.at[d_of[o], zz], up_g.at[d, :, pl.ds(zz * TILE, TILE)], up_slots[o], dp_peer[o]
                ).start()
        for zz in range(4):
            pltpu.make_async_copy(up.at[d, zz], up_g.at[d, :, pl.ds(zz * TILE, TILE)], loc_sem.at[1]).start()

    dk_t = jnp.zeros((HD, SEQ), F32)
    dv_t = jnp.zeros((HD, SEQ), F32)
    dq_list = []
    for j in range(2):
        grad = dctx[:, j * HD:(j + 1) * HD]
        grad_low = grad.astype(BF16)
        pr = probs[j]
        dp = dot_nn(grad_low, v_t)
        ds = (pr * (dp - jnp.sum(dp * pr, axis=1, keepdims=True)) * SCALE).astype(BF16)
        dq = dot_nt(k_t, ds)
        dq_list.append(dq * cos_t - swap_rows(dq) * sin_t)
        dk_t += dot_nn(jnp.transpose(qs[j].astype(F32)).astype(BF16), ds)
        dv_t += dot_nn(jnp.transpose(grad).astype(BF16), pr.astype(BF16))
    dk_t = dk_t * cos_t - swap_rows(dk_t) * sin_t
    for i in range(4):
        kvp_send[i, 0:32] = dk_t[i * 32:(i + 1) * 32].astype(BF16)
        kvp_send[i, 32:64] = dv_t[i * 32:(i + 1) * 32].astype(BF16)
    kvp_slots = [None] + [slot() for _ in range(3)]
    kvp_copies = [
        remote(kvp_send.at[ring(z + o)], kvp_recv.at[o], kvp_slots[o], z_peer[o]) for o in (1, 2, 3)
    ]
    for copy in kvp_copies:
        copy.start()
    inv_t = jnp.transpose(inv_ref[...])[0:1, :]
    dq_t = jnp.concatenate(dq_list, axis=0)
    dqkv[0:256, :] = (dq_t * inv_t).astype(BF16)
    dq = jnp.transpose(dq_t)
    aq[...] = (dq * inv).astype(BF16)
    stat = jnp.sum(dq * xq[...], axis=1, keepdims=True)
    for copy in kvp_copies:
        copy.wait_recv()
    dkv_t = kvp_send[z].astype(F32)
    for o in (1, 2, 3):
        dkv_t += kvp_recv[o].astype(F32)
    dqkv[256:320, :] = (dkv_t * inv_t).astype(BF16)
    dkv = jnp.transpose(dkv_t)
    akv[...] = (dkv * inv).astype(BF16)
    stat += jnp.sum(dkv * xkv[...], axis=1, keepdims=True)
    cs_ref[...] = jnp.broadcast_to(inv * inv * inv * stat * (1.0 / D), cs_ref.shape)
    d_slots = [None] + [slot() for _ in range(3)]
    d_copies = [remote(dqkv, d_g.at[d], d_slots[o], dp_peer[o]) for o in (1, 2, 3)]
    d_keep = pltpu.make_async_copy(dqkv, d_g.at[d], loc_sem.at[3])
    for copy in d_copies:
        copy.start()
    d_keep.start()

    ring_of, other_of = (y, z), (z, y)
    right_1, left_1 = (y_right, z_right), (y_left, z_left)
    right_2, left_2 = (z_right, y_right), (z_left, y_left)

    def block(k, a, lo, n):
        if k == 0:
            return part.at[a, pl.ds(lo, n), halves(k), :]
        return part.at[pl.ds(lo, n), a, halves(k), :]

    def tile(k, a, b):
        return (a, b) if k == 0 else (b, a)

    def compute(k, a):
        def body(b, carry):
            yy, zz = tile(k, a, b)
            span = wo_rows(yy, zz)
            total = dot_nt(aq[halves(k), :], wq[span, :]) + dot_nn(akv[halves(k), :], wkv[:, span])
            total = total * gain[0:1, span].astype(F32) - tok[halves(k), span].astype(F32) * cs_ref[halves(k), 0:1]
            part[yy, zz, halves(k), :] = total.astype(BF16)
            return carry

        lax.fori_loop(0, 4, body, 0)

    rs1 = [[slot() for _ in range(6)] for _ in range(2)]
    rs2 = [[slot() for _ in range(6)] for _ in range(2)]
    sent = []

    def go(src, dst, n, peer):
        copy = remote(src, dst, n, peer)
        copy.start()
        sent.append(copy)

    for k in range(2):
        i = ring_of[k]
        compute(k, ring(i + 2))
        go(block(k, ring(i + 2), 0, 2), rrel.at[k, 0:2], rs1[k][0], right_1[k])
        go(block(k, ring(i + 2), 2, 2), rrel.at[k, 2:4], rs1[k][1], left_1[k])
    for k in range(2):
        i = ring_of[k]
        compute(k, ring(i + 1))
        go(block(k, ring(i + 1), 2, 2), rdir.at[k, 2:4], rs1[k][5], right_1[k])
        compute(k, ring(i - 1))
        go(block(k, ring(i - 1), 0, 2), rdir.at[k, 0:2], rs1[k][4], left_1[k])
    for k in range(2):
        compute(k, ring_of[k])

    def landed(ref, n):
        remote(ref, ref, n, y_right).wait_recv()

    for k in range(2):
        i = ring_of[k]
        landed(rrel.at[k, 0:2], rs1[k][0])
        for b in range(2):
            yy, zz = tile(k, ring(i + 1), b)
            part[yy, zz, halves(k), :] = (
                part[yy, zz, halves(k), :].astype(F32) + rrel[k, b].astype(F32)
            ).astype(BF16)
        go(block(k, ring(i + 1), 0, 2), racc.at[k, 0:2], rs1[k][2], right_1[k])
        landed(rrel.at[k, 2:4], rs1[k][1])
        for b in range(2, 4):
            yy, zz = tile(k, ring(i - 1), b)
            part[yy, zz, halves(k), :] = (
                part[yy, zz, halves(k), :].astype(F32) + rrel[k, b].astype(F32)
            ).astype(BF16)
        go(block(k, ring(i - 1), 2, 2), racc.at[k, 2:4], rs1[k][3], left_1[k])

    def collect(k, b):
        yy, zz = tile(k, ring_of[k], b)
        summed[k, b] = (
            part[yy, zz, halves(k), :].astype(F32) + racc[k, b].astype(F32) + rdir[k, b].astype(F32)
        ).astype(BF16)

    for k in range(2):
        j = other_of[k]
        landed(rdir.at[k, 0:2], rs1[k][4])
        landed(rdir.at[k, 2:4], rs1[k][5])
        landed(racc.at[k, 0:2], rs1[k][2])
        landed(racc.at[k, 2:4], rs1[k][3])
        collect(k, ring(j + 2))
        go(summed.at[k, ring(j + 2), 0:64], rrel2.at[k, 0:64], rs2[k][0], right_2[k])
        go(summed.at[k, ring(j + 2), 64:128], rrel2.at[k, 64:128], rs2[k][1], left_2[k])
        collect(k, ring(j + 1))
        go(summed.at[k, ring(j + 1), 64:128], rdir2.at[k, 64:128], rs2[k][5], right_2[k])
        collect(k, ring(j - 1))
        go(summed.at[k, ring(j - 1), 0:64], rdir2.at[k, 0:64], rs2[k][4], left_2[k])
        collect(k, j)
    for k in range(2):
        j = other_of[k]
        landed(rrel2.at[k, 0:64], rs2[k][0])
        a = ring(j + 1)
        summed[k, a, 0:64] = (summed[k, a, 0:64].astype(F32) + rrel2[k, 0:64].astype(F32)).astype(BF16)
        go(summed.at[k, a, 0:64], racc2.at[k, 0:64], rs2[k][2], right_2[k])
        landed(rrel2.at[k, 64:128], rs2[k][1])
        a = ring(j - 1)
        summed[k, a, 64:128] = (summed[k, a, 64:128].astype(F32) + rrel2[k, 64:128].astype(F32)).astype(BF16)
        go(summed.at[k, a, 64:128], racc2.at[k, 64:128], rs2[k][3], left_2[k])
    for k in range(2):
        j = other_of[k]
        landed(rdir2.at[k, 0:64], rs2[k][4])
        landed(rdir2.at[k, 64:128], rs2[k][5])
        landed(racc2.at[k, 0:64], rs2[k][2])
        landed(racc2.at[k, 64:128], rs2[k][3])
        gin[halves(k), :] = (
            up[y, z, halves(k), :].astype(F32)
            + summed[k, j].astype(F32)
            + racc2[k].astype(F32)
            + rdir2[k].astype(F32)
        ).astype(BF16)

        @pl.when(is_later)
        def _():
            remote(gin.at[halves(k), :], up.at[y, z, halves(k), :], own_slots[k], hand_peer).start()

    for copy in sent + kv_copies + ctx_copies + kvp_copies + d_copies:
        copy.wait_send()
    for copy in ctx_copies + d_copies:
        copy.wait_recv()
    ctx_keep.wait()
    d_keep.wait()

    @pl.when(is_later)
    def _():
        for k in range(2):
            hand_copy(k).wait_send()

    tok_keep(late).wait()
    cot_keep().wait()
    for o in (1, 2, 3):
        copy = tok_send(late, o)
        copy.wait_send()
        copy.wait_recv()
        copy = cot_send(o)
        copy.wait_recv()

    @pl.when(is_later)
    def _():
        cot_send(1).wait_send()

    @pl.when(is_earlier)
    def _():
        for o in (1, 2, 3):
            cot_send(o).wait_send()
        for o in (2, 3):
            cot_send(o).wait_send()


N_SLOTS = 6 + 3 + 3 + 2 + 8 + 32 + 3 + 3 + 24


def relay(late, cot, early, lens, gain, w_q, w_k, w_v, w_o, freq):
    any_spec = pl.BlockSpec(memory_space=pl.ANY)
    vmem = pl.BlockSpec(memory_space=pltpu.VMEM)
    smem = pl.BlockSpec(memory_space=pltpu.SMEM)
    out_shape = (
        jax.ShapeDtypeStruct((SEQ, TILE), BF16),
        jax.ShapeDtypeStruct((4, SEQ, BLOCK), BF16),
        jax.ShapeDtypeStruct((4, SEQ, BLOCK), BF16),
        jax.ShapeDtypeStruct((4, ROWS, SEQ), BF16),
        jax.ShapeDtypeStruct((4, SEQ, SEQ), BF16),
    )
    scratch = [
        pltpu.VMEM((SEQ, D), BF16),
        pltpu.VMEM((D, 256), BF16),
        pltpu.VMEM((KV, D), BF16),
        pltpu.VMEM((D, 256), BF16),
        pltpu.VMEM((4, 4, SEQ, TILE), BF16),
        pltpu.VMEM((4, 4, SEQ, TILE), BF16),
        pltpu.VMEM((SEQ, 256), F32),
        pltpu.VMEM((SEQ, KV), F32),
        pltpu.VMEM((SEQ, 256), F32),
        pltpu.VMEM((2, SEQ, SEQ), F32),
        pltpu.VMEM((2, SEQ, HD), BF16),
        pltpu.VMEM((4, KV, SEQ), BF16),
        pltpu.VMEM((4, KV, SEQ), BF16),
        pltpu.VMEM((4, KV, SEQ), BF16),
        pltpu.VMEM((SEQ, HD), F32),
        pltpu.VMEM((SEQ, HD), F32),
        pltpu.VMEM((SEQ, HD), F32),
        pltpu.VMEM((SEQ, HD), F32),
        pltpu.VMEM((SEQ, 256), BF16),
        pltpu.VMEM((SEQ, KV), BF16),
        pltpu.VMEM((ROWS, SEQ), BF16),
        pltpu.VMEM((256, SEQ), BF16),
        pltpu.VMEM((2, 4, 128, TILE), BF16),
        pltpu.VMEM((2, 4, 128, TILE), BF16),
        pltpu.VMEM((2, 4, 128, TILE), BF16),
        pltpu.VMEM((2, 4, 128, TILE), BF16),
        pltpu.VMEM((2, 128, TILE), BF16),
        pltpu.VMEM((2, 128, TILE), BF16),
        pltpu.VMEM((2, 128, TILE), BF16),
        pltpu.SemaphoreType.DMA((5, N_CHUNK)),
        pltpu.SemaphoreType.DMA((4, 4)),
        pltpu.SemaphoreType.DMA((4,)),
        pltpu.SemaphoreType.DMA((N_SLOTS,)),
        pltpu.SemaphoreType.DMA((N_SLOTS,)),
    ]
    return pl.pallas_call(
        relay_kernel,
        out_shape=out_shape,
        in_specs=[any_spec, any_spec, any_spec, smem, vmem, any_spec, any_spec, any_spec, any_spec, vmem],
        out_specs=(vmem, any_spec, any_spec, any_spec, any_spec),
        scratch_shapes=scratch,
        compiler_params=pltpu.CompilerParams(
            collective_id=0, has_side_effects=True, vmem_limit_bytes=52 * 1024 * 1024
        ),
        name="relay",
    )(late, cot, early, lens, gain, w_q, w_k, w_v, w_o, freq)


def weights_kernel(tok, up, d_ref, c_ref, gain, gin, q_out, o_out, k_out, v_out, gin_out):
    i = pl.program_id(0)
    start = pl.multiple_of(lax.axis_index("dp") * BLOCK + i * TILE, TILE)
    total = dot_nn(d_ref[0], tok[0])
    for e in range(1, 4):
        total += dot_nn(d_ref[e], tok[e])
    total = total * gain[0:1, pl.ds(start, TILE)].astype(F32)
    q_out[...] = jnp.transpose(total[0:256]).astype(BF16)
    k_out[...] = total[256:288].astype(BF16)
    v_out[...] = total[288:320].astype(BF16)
    other = dot_nn(c_ref[0], up[0])
    for e in range(1, 4):
        other += dot_nn(c_ref[e], up[e])
    o_out[...] = jnp.transpose(other).astype(BF16)
    gin_out[...] = gin[...]


def weight_grads(tok_g, up_g, d_g, c_g, gain, gin):
    return pl.pallas_call(
        weights_kernel,
        grid=(4,),
        out_shape=(
            jax.ShapeDtypeStruct((BLOCK, 256), BF16),
            jax.ShapeDtypeStruct((BLOCK, 256), BF16),
            jax.ShapeDtypeStruct((32, BLOCK), BF16),
            jax.ShapeDtypeStruct((32, BLOCK), BF16),
            jax.ShapeDtypeStruct((SEQ, TILE), BF16),
        ),
        in_specs=[
            pl.BlockSpec((4, SEQ, TILE), lambda i: (0, 0, i)),
            pl.BlockSpec((4, SEQ, TILE), lambda i: (0, 0, i)),
            pl.BlockSpec((4, ROWS, SEQ), lambda i: (0, 0, 0)),
            pl.BlockSpec((4, SEQ, SEQ), lambda i: (0, 0, 0)),
            pl.BlockSpec((1, D), lambda i: (0, 0)),
            pl.BlockSpec((SEQ, TILE), lambda i: (0, 0)),
        ],
        out_specs=(
            pl.BlockSpec((TILE, 256), lambda i: (i, 0)),
            pl.BlockSpec((TILE, 256), lambda i: (i, 0)),
            pl.BlockSpec((32, TILE), lambda i: (0, i)),
            pl.BlockSpec((32, TILE), lambda i: (0, i)),
            pl.BlockSpec((SEQ, TILE), lambda i: (0, 0)),
        ),
        compiler_params=pltpu.CompilerParams(vmem_limit_bytes=40 * 1024 * 1024),
        name="weight_grads",
    )(tok_g, up_g, d_g, c_g, gain, gin)


def on_device(
    late_inputs, cotangent, early_inputs, doc_lengths, norm_gain, w_query, w_key, w_value, w_output
):
    half = 10000.0 ** (-np.arange(0, HD, 2).astype(np.float32) / HD)
    freq = jnp.asarray(np.concatenate([half, half]).astype(np.float32)[None, :])
    gin, tok_g, up_g, d_g, c_g = relay(
        late_inputs, cotangent, early_inputs, doc_lengths, norm_gain,
        w_query[0], w_key[0].T, w_value[0].T, w_output[0], freq,
    )
    grad_q, grad_o, grad_k, grad_v, grad_in = weight_grads(tok_g, up_g, d_g, c_g, norm_gain, gin)
    return grad_in[None], grad_q[None], grad_k.T[None], grad_v.T[None], grad_o[None]


def solution(mesh):
    in_specs = (
        P("dp", None),
        P("dp", None),
        P("dp", None),
        P("dp", None),
        P("section", None),
        P("section", None, "mp"),
        P("section", None, "mp"),
        P("section", None, "mp"),
        P("section", None, "mp"),
    )
    out_specs = (P("section", "dp", "mp"),) * 5
    return jax.shard_map(
        on_device, mesh=mesh, in_specs=in_specs, out_specs=out_specs, check_vma=False
    )
```

```python
import functools
import math

import jax
import jax.numpy as jnp
import numpy as np
from jax import lax
from jax.experimental import pallas as pl
from jax.experimental.pallas import tpu as pltpu
from jax.sharding import PartitionSpec as P

HD = 128
SEQ = 256
D = 8192
TILE = 512
BLOCK = 2048
KV = 64
ROWS = 320
CHUNK = 1024
N_CHUNK = D // CHUNK
SCALE = 1.0 / math.sqrt(HD)
F32 = jnp.float32
BF16 = jnp.bfloat16
MESH = pl.DeviceIdType.MESH


def dot_nn(a, b):
    return lax.dot_general(a, b, (((1,), (0,)), ((), ())), preferred_element_type=F32)


def dot_nt(a, b):
    return lax.dot_general(a, b, (((1,), (1,)), ((), ())), preferred_element_type=F32)


def ring(v):
    return lax.rem(v + 4, 4)


def begin_of(lens, places):
    start = jnp.int32(0)
    begins = jnp.zeros_like(places)
    for i in range(4):
        begins = jnp.maximum(begins, jnp.where(places >= start, start, 0))
        start = start + lens[0, i]
    return begins


def swap_rows(v):
    return jnp.concatenate([v[64:128], v[0:64]], axis=0)


def relay_kernel(
    late, cot, early, lens, gain, w_q, w_k, w_v, w_o, freq,
    gin, tok_g, up_g, d_g, c_g,
    tok, wq, wkv, wo, up, part,
    xq, xkv, dctx, probs, dss, qs, qs_t, kv_all, kvp_send, kvp_recv, cosv, sinv, inv_ref, cs_ref,
    aq, akv, dqkv, ctx,
    rrel, racc, rdir, summed, rrel2, racc2, rdir2, hop, stage, cot_stage, cot_part,
    load_sem, up_sem, stage_sem, loc_sem, send_sem, recv_sem,
):
    s = lax.axis_index("section")
    d = lax.axis_index("dp")
    m = lax.axis_index("mp")
    y, z = lax.div(m, 4), lax.rem(m, 4)
    h, c = lax.div(d, 2), lax.rem(d, 2)
    d_of = [d, h * 2 + (1 - c), (1 - h) * 2 + c, (1 - h) * 2 + (1 - c)]
    is_later = s == 1
    is_earlier = s == 0

    def mp_id(yy, zz):
        return {"mp": yy * 4 + zz}

    z_peer = [mp_id(y, ring(z + o)) for o in range(4)]
    y_right, y_left = mp_id(ring(y + 1), z), mp_id(ring(y - 1), z)
    z_right, z_left = z_peer[1], z_peer[3]
    dp_peer = [{"dp": d_of[o]} for o in range(4)]
    cross_peer = [None, None] + [{"section": 1 - s, "dp": d_of[o]} for o in (2, 3)]
    hand_peer = {"section": 1 - s}

    def tok_copy(source, i):
        return pltpu.make_async_copy(
            source.at[:, pl.ds(i * CHUNK, CHUNK)], tok.at[:, pl.ds(i * CHUNK, CHUNK)], load_sem.at[0, i]
        )

    def wq_copy(i):
        return pltpu.make_async_copy(
            w_q.at[pl.ds(i * CHUNK, CHUNK), :], wq.at[pl.ds(i * CHUNK, CHUNK), :], load_sem.at[1, i]
        )

    wk_copy = pltpu.make_async_copy(w_k, wkv.at[0:32, :], load_sem.at[2, 0])
    wv_copy = pltpu.make_async_copy(w_v, wkv.at[32:64, :], load_sem.at[3, 0])

    def wo_copy(i):
        return pltpu.make_async_copy(
            w_o.at[pl.ds(i * CHUNK, CHUNK), :], wo.at[pl.ds(i * CHUNK, CHUNK), :], load_sem.at[4, i]
        )

    def cot_copy(yy, zz):
        return pltpu.make_async_copy(
            cot.at[:, pl.ds(pl.multiple_of((yy * 4 + zz) * TILE, TILE), TILE)], up.at[yy, zz], up_sem.at[yy, zz]
        )

    def per_section(later, earlier):
        pl.when(is_later)(later)
        pl.when(is_earlier)(earlier)

    wk_copy.start()
    wv_copy.start()
    for i in range(N_CHUNK):
        per_section(lambda: tok_copy(late, i).start(), lambda: tok_copy(early, i).start())
    for i in range(N_CHUNK):
        wq_copy(i).start()

    def cols(index):
        return pl.ds(pl.multiple_of(index * BLOCK, BLOCK), BLOCK)

    def quarter(index, zz):
        return pl.ds(pl.multiple_of(index * BLOCK + zz * TILE, TILE), TILE)

    def stage_copy(source, o):
        return pltpu.make_async_copy(source.at[:, cols(d_of[o])], stage.at[o - 2], stage_sem.at[0, o - 2])

    def cot_stage_copy(o):
        return pltpu.make_async_copy(
            cot.at[:, quarter(d_of[o], z)], cot_stage.at[o - 2], stage_sem.at[1, o - 2]
        )

    def load_rest():
        for i in range(N_CHUNK):
            wo_copy(i).start()

        @pl.when(is_later)
        def _():
            for yy in range(4):
                for zz in range(4):
                    cot_copy(yy, zz).start()

        @pl.when(is_earlier)
        def _():
            for o in (2, 3):
                cot_stage_copy(o).start()

        for o in (2, 3):
            per_section(lambda: stage_copy(early, o).start(), lambda: stage_copy(late, o).start())

    barrier = pltpu.get_barrier_semaphore()
    greeted = [z_peer[1], z_peer[2], z_peer[3], y_right, y_left, hand_peer]
    greeted += dp_peer[1:] + cross_peer[2:]
    for peer in greeted:
        pl.semaphore_signal(barrier, inc=1, device_id=peer, device_id_type=MESH)

    count = [0]

    def slot():
        count[0] += 1
        return count[0] - 1

    def remote(src, dst, n, peer):
        return pltpu.make_async_remote_copy(
            src_ref=src, dst_ref=dst, send_sem=send_sem.at[n], recv_sem=recv_sem.at[n],
            device_id=peer, device_id_type=MESH,
        )

    xkv[...] = jnp.zeros_like(xkv)
    inv_ref[...] = jnp.zeros_like(inv_ref)

    def scaled(span):
        return (tok[:, span].astype(F32) * gain[0:1, span].astype(F32)).astype(BF16)

    def project_kv(i, carry):
        span = pl.ds(pl.multiple_of(i * CHUNK, CHUNK), CHUNK)
        tok_copy(late, i).wait()
        t = tok[:, span].astype(F32)
        inv_ref[...] += jnp.sum(t * t, axis=1, keepdims=True)
        xkv[...] += dot_nt(scaled(span), wkv[:, span])
        return carry

    wk_copy.wait()
    wv_copy.wait()
    lax.fori_loop(0, N_CHUNK, project_kv, 0, unroll=2)
    inv_ref[...] = lax.rsqrt(inv_ref[...] * (1.0 / D) + 1e-5)
    inv = inv_ref[:, 0:1]

    kv_all[z] = jnp.transpose(xkv[...] * inv).astype(BF16)
    pl.semaphore_wait(barrier, len(greeted))
    kv_slots = [None] + [slot() for _ in range(3)]
    kv_copies = [remote(kv_all.at[z], kv_all.at[z], kv_slots[o], z_peer[o]) for o in (1, 2, 3)]
    for copy in kv_copies:
        copy.start()

    tok_slots = [None] + [slot() for _ in range(3)]
    up_slots = [None] + [slot() for _ in range(3)]
    cot_slots = [None, None, slot(), slot()]
    share_slots = [[slot() for _ in range(3)] for _ in range(2)]

    def tok_send(o):
        if o == 1:
            return remote(tok.at[:, cols(d_of[1])], tok_g.at[d], tok_slots[1], dp_peer[1])
        return remote(stage.at[o - 2], tok_g.at[d], tok_slots[o], cross_peer[o])

    def tok_keep():
        return pltpu.make_async_copy(tok.at[:, cols(d)], tok_g.at[d], loc_sem.at[0])

    def up_send(o, zz):
        return remote(up.at[d_of[o], zz], up_g.at[d, :, quarter(0, zz)], up_slots[o], dp_peer[o])

    def up_keep(zz):
        return pltpu.make_async_copy(up.at[d, zz], up_g.at[d, :, quarter(0, zz)], loc_sem.at[1])

    def whole_block(o):
        return remote(stage.at[0], up_g.at[d], up_slots[o], dp_peer[o])

    def whole_keep():
        return pltpu.make_async_copy(stage.at[0], up_g.at[d], loc_sem.at[1])

    def cot_quarter(o):
        return remote(cot_stage.at[o - 2], cot_part.at[o - 2], cot_slots[o], cross_peer[o])

    def cot_share(o, p):
        return remote(
            cot_part.at[o - 2], up_g.at[d_of[o], :, quarter(0, z)], share_slots[o - 2][p - 1], z_peer[p]
        )

    def cot_keep(o):
        return pltpu.make_async_copy(
            cot_part.at[o - 2], up_g.at[d_of[o], :, quarter(0, z)], loc_sem.at[o + 2]
        )

    def send_operands():
        @pl.when(is_earlier)
        def _():
            for o in (2, 3):
                cot_stage_copy(o).wait()
                cot_quarter(o).start()

        for o in (2, 3):
            stage_copy(early, o).wait()
            tok_send(o).start()
        tok_send(1).start()
        tok_keep().start()

    load_rest()
    sent = list(kv_copies)
    received = []

    def finish():
        for copy in sent:
            copy.wait_send()
        for copy in received:
            copy.wait()

        @pl.when(is_later)
        def _():
            for o in (2, 3):
                for p in (1, 2, 3):
                    cot_share(o, p).wait()
                cot_keep(o).wait()
                whole_block(o).wait_send()

        @pl.when(is_earlier)
        def _():
            for o in (2, 3):
                cot_quarter(o).wait_send()
                for i in range(8):
                    hop_send(o, i).wait_send()
                whole_block(o).wait_recv()

        whole_block(1).wait()
        whole_keep().wait()
        for o in (1, 2, 3):
            tok_send(o).wait()
        tok_keep().wait()

    hop_slots = [None, None] + [[slot() for _ in range(8)] for _ in range(2)]

    def hop_send(o, i):
        zz, low = i // 2, i % 2 == 0
        rows = pl.ds(0 if low else 128, 128)
        return remote(
            up.at[d_of[o], zz, rows, :], hop.at[o - 2, i], hop_slots[o][i], hand_peer if low else cross_peer[o]
        )

    def hop_on(o, i):
        zz, low = i // 2, i % 2 == 0
        rows = pl.ds(0 if low else 128, 128)
        home = d if low else d_of[o]
        return remote(
            hop.at[o - 2, i], up_g.at[home, rows, pl.ds(zz * TILE, TILE)], up_slots[o],
            cross_peer[o] if low else hand_peer,
        )

    lane = lax.broadcasted_iota(jnp.int32, (SEQ, HD), 1)
    place = lax.broadcasted_iota(jnp.int32, (SEQ, HD), 0)
    offset = (place - begin_of(lens, place)).astype(F32)
    angle = offset * freq[0:1, :]
    cosv[...] = jnp.cos(angle)
    sinv[...] = jnp.where(lane < 64, -1.0, 1.0) * jnp.sin(angle)

    xq[...] = jnp.zeros_like(xq)

    def project_q(i, carry):
        span = pl.ds(pl.multiple_of(i * CHUNK, CHUNK), CHUNK)
        wq_copy(i).wait()
        xq[...] += dot_nn(scaled(span), wq[span, :])
        return carry

    lax.fori_loop(0, N_CHUNK, project_q, 0, unroll=2)
    cos = cosv[...]
    sin = sinv[...]
    cos_t = jnp.transpose(cos)
    sin_t = jnp.transpose(sin)
    for j in range(2):
        q = xq[:, j * HD:(j + 1) * HD] * inv
        q = q * cos + pltpu.roll(q, 64, 1) * sin
        qs[j] = q.astype(BF16)
        qs_t[j] = jnp.transpose(q).astype(BF16)
    inv_t = jnp.transpose(inv_ref[...])[0:1, :]
    for copy in kv_copies:
        copy.wait_recv()
    k = jnp.concatenate([kv_all[i, 0:32] for i in range(4)], axis=0).astype(F32)
    k_t = (k * cos_t + swap_rows(k) * sin_t).astype(BF16)
    v_t = jnp.concatenate([kv_all[i, 32:64] for i in range(4)], axis=0)

    row = lax.broadcasted_iota(jnp.int32, (SEQ, SEQ), 0)
    col = lax.broadcasted_iota(jnp.int32, (SEQ, SEQ), 1)
    allowed = (begin_of(lens, row) == begin_of(lens, col)) & (col <= row)
    for j in range(2):
        scores = jnp.where(allowed, dot_nn(qs[j], k_t) * SCALE, -1e30)
        peak = jnp.max(scores, axis=1, keepdims=True)
        ex = jnp.exp(scores - peak)
        pr = ex / jnp.sum(ex, axis=1, keepdims=True)
        probs[j] = pr
        ctx[j * HD:(j + 1) * HD, :] = dot_nt(v_t, pr.astype(BF16)).astype(BF16)
    ctx_slots = [None] + [slot() for _ in range(3)]
    ctx_copies = [remote(ctx, c_g.at[d], ctx_slots[o], dp_peer[o]) for o in (1, 2, 3)]
    ctx_keep = pltpu.make_async_copy(ctx, c_g.at[d], loc_sem.at[2])
    for copy in ctx_copies:
        copy.start()
    ctx_keep.start()
    received += ctx_copies + [ctx_keep]
    send_operands()

    for i in range(N_CHUNK):
        wo_copy(i).wait()
    dctx[...] = jnp.zeros_like(dctx)

    def wo_rows(yy, zz):
        return pl.ds(pl.multiple_of((yy * 4 + zz) * TILE, TILE), TILE)

    def halves(k):
        return pl.ds(k * 128, 128)

    def add_context(k, yy, zz):
        dctx[halves(k), :] += dot_nn(up[yy, zz, halves(k), :], wo[wo_rows(yy, zz), :])

    own_slots = [slot() for _ in range(4)]
    p1_slots = [[slot() for _ in range(4)] for _ in range(2)]
    p2_slots = [[[slot() for _ in range(4)] for _ in range(4)] for _ in range(2)]

    def rows_of(g):
        return pl.ds(g * 64, 64)

    def hand_copy(g):
        return remote(gin.at[rows_of(g), :], up.at[y, z, rows_of(g), :], own_slots[g], hand_peer)

    def at(k, first, second):
        return (second, first) if k == 0 else (first, second)

    @pl.when(is_later)
    def _():
        def body(yy, carry):
            total = dctx[...]
            for zz in range(4):
                cot_copy(yy, zz).wait()
            for zz in range(4):
                total += dot_nn(up[yy, zz], wo[wo_rows(yy, zz), :])
            dctx[...] = total
            return carry

        lax.fori_loop(0, 4, body, 0)

    @pl.when(is_earlier)
    def _():
        first_of, second_of = (z, y), (y, z)
        first_right, first_left = (z_right, y_right), (z_left, y_left)
        second_right, second_left = (y_right, z_right), (y_left, z_left)
        pending = []

        def piece(k, a, b, lo, n):
            yy, zz = at(k, a, b)
            return up.at[yy, zz, pl.ds(k * 128 + lo, n), :]

        def send(k, a, b, lo, n, index, peer):
            ref = piece(k, a, b, lo, n)
            copy = remote(ref, ref, index, peer)
            copy.start()
            pending.append(copy)

        def arrived(k, a, b, lo, n, index):
            ref = piece(k, a, b, lo, n)
            remote(ref, ref, index, hand_peer).wait_recv()

        def spread(k, o):
            a = ring(first_of[k] + o)
            send(k, a, second_of[k], 0, 128, p2_slots[k][o][0], second_right[k])
            send(k, a, second_of[k], 0, 128, p2_slots[k][o][1], second_left[k])

        for k in range(2):
            hand_copy(2 * k).wait_recv()
            hand_copy(2 * k + 1).wait_recv()
            send(k, first_of[k], second_of[k], 0, 128, p1_slots[k][0], first_right[k])
            send(k, first_of[k], second_of[k], 0, 128, p1_slots[k][1], first_left[k])
            spread(k, 0)
        for k in range(2):
            add_context(k, y, z)
        for k in range(2):
            a, b = ring(first_of[k] - 1), second_of[k]
            arrived(k, a, b, 0, 128, p1_slots[k][0])
            send(k, a, b, 0, 64, p1_slots[k][2], first_right[k])
            spread(k, 3)
            a = ring(first_of[k] + 1)
            arrived(k, a, b, 0, 128, p1_slots[k][1])
            send(k, a, b, 64, 64, p1_slots[k][3], first_left[k])
            spread(k, 1)
        for k in range(2):
            for o in (3, 1):
                add_context(k, *at(k, ring(first_of[k] + o), second_of[k]))

        def relay(k, o):
            a = ring(first_of[k] + o)
            left, right = ring(second_of[k] - 1), ring(second_of[k] + 1)
            arrived(k, a, left, 0, 128, p2_slots[k][o][0])
            send(k, a, left, 0, 64, p2_slots[k][o][2], second_right[k])
            arrived(k, a, right, 0, 128, p2_slots[k][o][1])
            send(k, a, right, 64, 64, p2_slots[k][o][3], second_left[k])
            add_context(k, *at(k, a, left))
            add_context(k, *at(k, a, right))

        for k in range(2):
            relay(k, 0)
        for k in range(2):
            a, b = ring(first_of[k] + 2), second_of[k]
            arrived(k, a, b, 0, 64, p1_slots[k][2])
            arrived(k, a, b, 64, 64, p1_slots[k][3])
            spread(k, 2)
            add_context(k, *at(k, a, b))
        for o in (3, 1, 2):
            for k in range(2):
                relay(k, o)
        for o in (0, 3, 1, 2):
            for k in range(2):
                a, b = ring(first_of[k] + o), ring(second_of[k] + 2)
                arrived(k, a, b, 0, 64, p2_slots[k][o][2])
                arrived(k, a, b, 64, 64, p2_slots[k][o][3])
                add_context(k, *at(k, a, b))
        for copy in pending:
            copy.wait_send()
        for i in range(8):
            for o in (2, 3):
                hop_send(o, i).start()

    for zz in range(4):
        up_send(1, zz).start()
        up_keep(zz).start()

    dk_t = jnp.zeros((HD, SEQ), F32)
    dv_t = jnp.zeros((HD, SEQ), F32)
    for j in range(2):
        grad = dctx[:, j * HD:(j + 1) * HD]
        pr = probs[j]
        dp = dot_nn(grad.astype(BF16), v_t)
        dss[j] = (pr * (dp - jnp.sum(dp * pr, axis=1, keepdims=True)) * SCALE).astype(BF16)
        dk_t += dot_nn(qs_t[j], dss[j])
        dv_t += dot_nn(jnp.transpose(grad).astype(BF16), pr.astype(BF16))
    dk_t = dk_t * cos_t - swap_rows(dk_t) * sin_t
    for i in range(4):
        kvp_send[i, 0:32] = dk_t[i * 32:(i + 1) * 32].astype(BF16)
        kvp_send[i, 32:64] = dv_t[i * 32:(i + 1) * 32].astype(BF16)
    kvp_slots = [None] + [slot() for _ in range(3)]
    kvp_copies = [
        remote(kvp_send.at[ring(z + o)], kvp_recv.at[o], kvp_slots[o], z_peer[o]) for o in (1, 2, 3)
    ]
    for copy in kvp_copies:
        copy.start()
    sent += kvp_copies
    dq_list = []
    for j in range(2):
        dq = dot_nt(k_t, dss[j])
        dq_list.append(dq * cos_t - swap_rows(dq) * sin_t)
    dq_t = jnp.concatenate(dq_list, axis=0)
    dqkv[0:256, :] = (dq_t * inv_t).astype(BF16)
    dq = jnp.transpose(dq_t)
    aq[...] = (dq * inv).astype(BF16)
    stat = jnp.sum(dq * xq[...], axis=1, keepdims=True)
    for copy in kvp_copies:
        copy.wait_recv()
    dkv_t = kvp_send[z].astype(F32)
    for o in (1, 2, 3):
        dkv_t += kvp_recv[o].astype(F32)
    dqkv[256:320, :] = (dkv_t * inv_t).astype(BF16)
    dkv = jnp.transpose(dkv_t)
    akv[...] = (dkv * inv).astype(BF16)
    stat += jnp.sum(dkv * xkv[...], axis=1, keepdims=True)
    cs_ref[...] = jnp.broadcast_to(inv * inv * inv * stat * (1.0 / D), cs_ref.shape)
    d_slots = [None] + [slot() for _ in range(3)]
    d_copies = [remote(dqkv, d_g.at[d], d_slots[o], dp_peer[o]) for o in (1, 2, 3)]
    d_keep = pltpu.make_async_copy(dqkv, d_g.at[d], loc_sem.at[3])
    for copy in d_copies:
        copy.start()
    d_keep.start()
    received += d_copies + [d_keep]

    ring_of, other_of = (y, z), (z, y)
    right_1, left_1 = (y_right, z_right), (y_left, z_left)
    right_2, left_2 = (z_right, y_right), (z_left, y_left)

    def block(g, a, lo, n):
        if g < 2:
            return part.at[a, pl.ds(lo, n), rows_of(g), :]
        return part.at[pl.ds(lo, n), a, rows_of(g), :]

    def tile(k, a, b):
        return (a, b) if k == 0 else (b, a)

    def compute(*tiles):
        for dy, dz in tiles:
            yy, zz = ring(y + dy), ring(z + dz)
            span = wo_rows(yy, zz)
            total = dot_nt(aq[...], wq[span, :]) + dot_nn(akv[...], wkv[:, span])
            total = total * gain[0:1, span].astype(F32) - tok[:, span].astype(F32) * cs_ref[:, 0:1]
            part[yy, zz] = total.astype(BF16)

    rs1 = [[slot() for _ in range(6)] for _ in range(4)]
    rs2 = [[slot() for _ in range(6)] for _ in range(4)]

    def go(src, dst, n, peer):
        copy = remote(src, dst, n, peer)
        copy.start()
        sent.append(copy)

    def landed(ref, n):
        remote(ref, ref, n, y_right).wait_recv()

    def relay_1(g):
        k, i = g // 2, ring_of[g // 2]
        go(block(g, ring(i + 2), 0, 2), rrel.at[g, 0:2], rs1[g][0], right_1[k])
        go(block(g, ring(i + 2), 2, 2), rrel.at[g, 2:4], rs1[g][1], left_1[k])

    def direct_right_1(g):
        k, i = g // 2, ring_of[g // 2]
        go(block(g, ring(i + 1), 2, 2), rdir.at[g, 2:4], rs1[g][5], right_1[k])

    def direct_left_1(g):
        k, i = g // 2, ring_of[g // 2]
        go(block(g, ring(i - 1), 0, 2), rdir.at[g, 0:2], rs1[g][4], left_1[k])

    def add_relay(g, a, b):
        yy, zz = tile(g // 2, a, b)
        part[yy, zz, rows_of(g), :] = (
            part[yy, zz, rows_of(g), :].astype(F32) + rrel[g, b].astype(F32)
        ).astype(BF16)

    def accumulate_1(g):
        k, i = g // 2, ring_of[g // 2]
        landed(rrel.at[g, 0:2], rs1[g][0])
        for b in range(2):
            add_relay(g, ring(i + 1), b)
        go(block(g, ring(i + 1), 0, 2), racc.at[g, 0:2], rs1[g][2], right_1[k])
        landed(rrel.at[g, 2:4], rs1[g][1])
        for b in range(2, 4):
            add_relay(g, ring(i - 1), b)
        go(block(g, ring(i - 1), 2, 2), racc.at[g, 2:4], rs1[g][3], left_1[k])

    def collect(g, b):
        yy, zz = tile(g // 2, ring_of[g // 2], b)
        summed[g, b] = (
            part[yy, zz, rows_of(g), :].astype(F32) + racc[g, b].astype(F32) + rdir[g, b].astype(F32)
        ).astype(BF16)

    def turn(g):
        k, j = g // 2, other_of[g // 2]
        landed(rdir.at[g, 0:2], rs1[g][4])
        landed(rdir.at[g, 2:4], rs1[g][5])
        landed(racc.at[g, 0:2], rs1[g][2])
        landed(racc.at[g, 2:4], rs1[g][3])
        collect(g, ring(j + 2))
        go(summed.at[g, ring(j + 2), 0:32], rrel2.at[g, 0:32], rs2[g][0], right_2[k])
        go(summed.at[g, ring(j + 2), 32:64], rrel2.at[g, 32:64], rs2[g][1], left_2[k])
        collect(g, ring(j + 1))
        go(summed.at[g, ring(j + 1), 32:64], rdir2.at[g, 32:64], rs2[g][5], right_2[k])
        collect(g, ring(j - 1))
        go(summed.at[g, ring(j - 1), 0:32], rdir2.at[g, 0:32], rs2[g][4], left_2[k])
        collect(g, j)

    def accumulate_2(g):
        k, j = g // 2, other_of[g // 2]
        landed(rrel2.at[g, 0:32], rs2[g][0])
        a = ring(j + 1)
        summed[g, a, 0:32] = (summed[g, a, 0:32].astype(F32) + rrel2[g, 0:32].astype(F32)).astype(BF16)
        go(summed.at[g, a, 0:32], racc2.at[g, 0:32], rs2[g][2], right_2[k])
        landed(rrel2.at[g, 32:64], rs2[g][1])
        a = ring(j - 1)
        summed[g, a, 32:64] = (summed[g, a, 32:64].astype(F32) + rrel2[g, 32:64].astype(F32)).astype(BF16)
        go(summed.at[g, a, 32:64], racc2.at[g, 32:64], rs2[g][3], left_2[k])

    def result(g):
        j = other_of[g // 2]
        landed(rdir2.at[g, 0:32], rs2[g][4])
        landed(rdir2.at[g, 32:64], rs2[g][5])
        landed(racc2.at[g, 0:32], rs2[g][2])
        landed(racc2.at[g, 32:64], rs2[g][3])
        gin[rows_of(g), :] = (
            up[y, z, rows_of(g), :].astype(F32)
            + summed[g, j].astype(F32)
            + racc2[g].astype(F32)
            + rdir2[g].astype(F32)
        ).astype(BF16)
        pl.when(is_later)(lambda: hand_copy(g).start())

    def each(step, *groups):
        for g in groups:
            step(g)

    compute((2, 2), (2, 1), (2, 3), (2, 0))
    each(relay_1, 0, 1)
    compute((1, 2), (3, 2), (0, 2))
    each(relay_1, 2, 3)
    compute((1, 1), (1, 3), (1, 0))
    direct_right_1(0)
    compute((3, 1), (3, 3), (3, 0))
    direct_left_1(0)
    compute((0, 1), (0, 3))
    each(direct_right_1, 2)
    each(direct_left_1, 2)
    each(accumulate_1, 0, 2)
    each(direct_right_1, 1, 3)
    each(direct_left_1, 1, 3)
    compute((0, 0))
    each(accumulate_1, 1, 3)
    each(turn, 0, 2)
    each(accumulate_2, 0, 2)
    each(turn, 1, 3)
    each(result, 0, 2)
    each(accumulate_2, 1, 3)
    each(result, 1, 3)

    @pl.when(is_later)
    def _():
        for o in (2, 3):
            cot_quarter(o).wait_recv()
            for p in (1, 2, 3):
                cot_share(o, p).start()
            cot_keep(o).start()
        for i in range(8):
            for o in (2, 3):
                hop_send(o, i).wait_recv()
                hop_on(o, i).start()
        for g in range(4):
            hand_copy(g).wait_send()

    finish()


N_SLOTS = 6 + 3 + 2 + 6 + 16 + 3 + 4 + 8 + 32 + 3 + 3 + 48


def relay(late, cot, early, lens, gain, w_q, w_k, w_v, w_o, freq):
    any_spec = pl.BlockSpec(memory_space=pl.ANY)
    vmem = pl.BlockSpec(memory_space=pltpu.VMEM)
    smem = pl.BlockSpec(memory_space=pltpu.SMEM)
    out_shape = (
        jax.ShapeDtypeStruct((SEQ, TILE), BF16),
        jax.ShapeDtypeStruct((4, SEQ, BLOCK), BF16),
        jax.ShapeDtypeStruct((4, SEQ, BLOCK), BF16),
        jax.ShapeDtypeStruct((4, ROWS, SEQ), BF16),
        jax.ShapeDtypeStruct((4, SEQ, SEQ), BF16),
    )
    scratch = [
        pltpu.VMEM((SEQ, D), BF16),
        pltpu.VMEM((D, 256), BF16),
        pltpu.VMEM((KV, D), BF16),
        pltpu.VMEM((D, 256), BF16),
        pltpu.VMEM((4, 4, SEQ, TILE), BF16),
        pltpu.VMEM((4, 4, SEQ, TILE), BF16),
        pltpu.VMEM((SEQ, 256), F32),
        pltpu.VMEM((SEQ, KV), F32),
        pltpu.VMEM((SEQ, 256), F32),
        pltpu.VMEM((2, SEQ, SEQ), F32),
        pltpu.VMEM((2, SEQ, SEQ), BF16),
        pltpu.VMEM((2, SEQ, HD), BF16),
        pltpu.VMEM((2, HD, SEQ), BF16),
        pltpu.VMEM((4, KV, SEQ), BF16),
        pltpu.VMEM((4, KV, SEQ), BF16),
        pltpu.VMEM((4, KV, SEQ), BF16),
        pltpu.VMEM((SEQ, HD), F32),
        pltpu.VMEM((SEQ, HD), F32),
        pltpu.VMEM((SEQ, HD), F32),
        pltpu.VMEM((SEQ, HD), F32),
        pltpu.VMEM((SEQ, 256), BF16),
        pltpu.VMEM((SEQ, KV), BF16),
        pltpu.VMEM((ROWS, SEQ), BF16),
        pltpu.VMEM((256, SEQ), BF16),
        pltpu.VMEM((4, 4, 64, TILE), BF16),
        pltpu.VMEM((4, 4, 64, TILE), BF16),
        pltpu.VMEM((4, 4, 64, TILE), BF16),
        pltpu.VMEM((4, 4, 64, TILE), BF16),
        pltpu.VMEM((4, 64, TILE), BF16),
        pltpu.VMEM((4, 64, TILE), BF16),
        pltpu.VMEM((4, 64, TILE), BF16),
        pltpu.VMEM((2, 8, 128, TILE), BF16),
        pltpu.VMEM((2, SEQ, BLOCK), BF16),
        pltpu.VMEM((2, SEQ, TILE), BF16),
        pltpu.VMEM((2, SEQ, TILE), BF16),
        pltpu.SemaphoreType.DMA((5, N_CHUNK)),
        pltpu.SemaphoreType.DMA((4, 4)),
        pltpu.SemaphoreType.DMA((2, 2)),
        pltpu.SemaphoreType.DMA((6,)),
        pltpu.SemaphoreType.DMA((N_SLOTS,)),
        pltpu.SemaphoreType.DMA((N_SLOTS,)),
    ]
    return pl.pallas_call(
        relay_kernel,
        out_shape=out_shape,
        in_specs=[any_spec, any_spec, any_spec, smem, vmem, any_spec, any_spec, any_spec, any_spec, vmem],
        out_specs=(vmem, any_spec, any_spec, any_spec, any_spec),
        scratch_shapes=scratch,
        compiler_params=pltpu.CompilerParams(
            collective_id=0, has_side_effects=True, vmem_limit_bytes=62 * 1024 * 1024
        ),
        name="relay",
    )(late, cot, early, lens, gain, w_q, w_k, w_v, w_o, freq)


def weights_kernel(tok, up, d_ref, c_ref, gain, gin, q_out, o_out, k_out, v_out, gin_out):
    i = pl.program_id(0)
    start = pl.multiple_of(lax.axis_index("dp") * BLOCK + i * TILE, TILE)
    total = dot_nn(d_ref[0], tok[0])
    for e in range(1, 4):
        total += dot_nn(d_ref[e], tok[e])
    total = total * gain[0:1, pl.ds(start, TILE)].astype(F32)
    q_out[...] = jnp.transpose(total[0:256]).astype(BF16)
    k_out[...] = total[256:288].astype(BF16)
    v_out[...] = total[288:320].astype(BF16)
    other = dot_nn(c_ref[0], up[0])
    for e in range(1, 4):
        other += dot_nn(c_ref[e], up[e])
    o_out[...] = jnp.transpose(other).astype(BF16)
    gin_out[...] = gin[...]


def weight_grads(tok_g, up_g, d_g, c_g, gain, gin):
    return pl.pallas_call(
        weights_kernel,
        grid=(4,),
        out_shape=(
            jax.ShapeDtypeStruct((BLOCK, 256), BF16),
            jax.ShapeDtypeStruct((BLOCK, 256), BF16),
            jax.ShapeDtypeStruct((32, BLOCK), BF16),
            jax.ShapeDtypeStruct((32, BLOCK), BF16),
            jax.ShapeDtypeStruct((SEQ, TILE), BF16),
        ),
        in_specs=[
            pl.BlockSpec((4, SEQ, TILE), lambda i: (0, 0, i)),
            pl.BlockSpec((4, SEQ, TILE), lambda i: (0, 0, i)),
            pl.BlockSpec((4, ROWS, SEQ), lambda i: (0, 0, 0)),
            pl.BlockSpec((4, SEQ, SEQ), lambda i: (0, 0, 0)),
            pl.BlockSpec((1, D), lambda i: (0, 0)),
            pl.BlockSpec((SEQ, TILE), lambda i: (0, 0)),
        ],
        out_specs=(
            pl.BlockSpec((TILE, 256), lambda i: (i, 0)),
            pl.BlockSpec((TILE, 256), lambda i: (i, 0)),
            pl.BlockSpec((32, TILE), lambda i: (0, i)),
            pl.BlockSpec((32, TILE), lambda i: (0, i)),
            pl.BlockSpec((SEQ, TILE), lambda i: (0, 0)),
        ),
        compiler_params=pltpu.CompilerParams(vmem_limit_bytes=62 * 1024 * 1024),
        name="weight_grads",
    )(tok_g, up_g, d_g, c_g, gain, gin)


def on_device(
    late_inputs, cotangent, early_inputs, doc_lengths, norm_gain, w_query, w_key, w_value, w_output
):
    half = 10000.0 ** (-np.arange(0, HD, 2).astype(np.float32) / HD)
    freq = jnp.asarray(np.concatenate([half, half]).astype(np.float32)[None, :])
    gin, tok_g, up_g, d_g, c_g = relay(
        late_inputs, cotangent, early_inputs, doc_lengths, norm_gain,
        w_query[0], w_key[0].T, w_value[0].T, w_output[0], freq,
    )
    grad_q, grad_o, grad_k, grad_v, grad_in = weight_grads(tok_g, up_g, d_g, c_g, norm_gain, gin)
    return grad_in[None], grad_q[None], grad_k.T[None], grad_v.T[None], grad_o[None]


def solution(mesh):
    in_specs = (
        P("dp", None),
        P("dp", None),
        P("dp", None),
        P("dp", None),
        P("section", None),
        P("section", None, "mp"),
        P("section", None, "mp"),
        P("section", None, "mp"),
        P("section", None, "mp"),
    )
    out_specs = (P("section", "dp", "mp"),) * 5
    return jax.shard_map(
        on_device, mesh=mesh, in_specs=in_specs, out_specs=out_specs, check_vma=False
    )
```

```python
import functools
import math

import jax
import jax.numpy as jnp
import numpy as np
from jax import lax
from jax.experimental import pallas as pl
from jax.experimental.pallas import tpu as pltpu
from jax.sharding import PartitionSpec as P

HD = 128
SEQ = 256
D = 8192
TILE = 512
BLOCK = 2048
KV = 64
ROWS = 320
CHUNK = 1024
N_CHUNK = D // CHUNK
SCALE = 1.0 / math.sqrt(HD)
F32 = jnp.float32
BF16 = jnp.bfloat16
MESH = pl.DeviceIdType.MESH


def dot_nn(a, b):
    return lax.dot_general(a, b, (((1,), (0,)), ((), ())), preferred_element_type=F32)


def dot_nt(a, b):
    return lax.dot_general(a, b, (((1,), (1,)), ((), ())), preferred_element_type=F32)


def ring(v):
    return lax.rem(v + 4, 4)


def begin_of(lens, places):
    start = jnp.int32(0)
    begins = jnp.zeros_like(places)
    for i in range(4):
        begins = jnp.maximum(begins, jnp.where(places >= start, start, 0))
        start = start + lens[0, i]
    return begins


def swap_rows(v):
    return jnp.concatenate([v[64:128], v[0:64]], axis=0)


def relay_kernel(
    late, cot, early, lens, gain, w_q, w_k, w_v, w_o, freq,
    gin, tok_g, up_g, d_g, c_g,
    tok, wq, wkv, wo, up, part,
    xq, xkv, dctx, probs, dss, qs, qs_t, kv_all, kvp_send, kvp_recv, cosv, sinv, inv_ref, cs_ref,
    aq, akv, dqkv, ctx,
    rrel, racc, rdir, summed, rrel2, racc2, rdir2, hop, tok_stage, tok_part, cot_stage, cot_part,
    load_sem, up_sem, stage_sem, loc_sem, send_sem, recv_sem,
):
    s = lax.axis_index("section")
    d = lax.axis_index("dp")
    m = lax.axis_index("mp")
    y, z = lax.div(m, 4), lax.rem(m, 4)
    h, c = lax.div(d, 2), lax.rem(d, 2)
    d_of = [d, h * 2 + (1 - c), (1 - h) * 2 + c, (1 - h) * 2 + (1 - c)]
    is_later = s == 1
    is_earlier = s == 0

    def mp_id(yy, zz):
        return {"mp": yy * 4 + zz}

    z_peer = [mp_id(y, ring(z + o)) for o in range(4)]
    y_peer = [mp_id(ring(y + o), z) for o in range(4)]
    y_right, y_left = y_peer[1], y_peer[3]
    z_right, z_left = z_peer[1], z_peer[3]
    dp_peer = [{"dp": d_of[o]} for o in range(4)]
    cross_peer = [None, None] + [{"section": 1 - s, "dp": d_of[o]} for o in (2, 3)]
    hand_peer = {"section": 1 - s}

    def tok_copy(source, i):
        return pltpu.make_async_copy(
            source.at[:, pl.ds(i * CHUNK, CHUNK)], tok.at[:, pl.ds(i * CHUNK, CHUNK)], load_sem.at[0, i]
        )

    def wq_copy(i):
        return pltpu.make_async_copy(
            w_q.at[pl.ds(i * CHUNK, CHUNK), :], wq.at[pl.ds(i * CHUNK, CHUNK), :], load_sem.at[1, i]
        )

    wk_copy = pltpu.make_async_copy(w_k, wkv.at[0:32, :], load_sem.at[2, 0])
    wv_copy = pltpu.make_async_copy(w_v, wkv.at[32:64, :], load_sem.at[3, 0])

    def wo_copy(i):
        return pltpu.make_async_copy(
            w_o.at[pl.ds(i * CHUNK, CHUNK), :], wo.at[pl.ds(i * CHUNK, CHUNK), :], load_sem.at[4, i]
        )

    def cot_copy(yy, zz):
        return pltpu.make_async_copy(
            cot.at[:, pl.ds(pl.multiple_of((yy * 4 + zz) * TILE, TILE), TILE)], up.at[yy, zz], up_sem.at[yy, zz]
        )

    def per_section(later, earlier):
        pl.when(is_later)(later)
        pl.when(is_earlier)(earlier)

    wk_copy.start()
    wv_copy.start()
    for i in range(N_CHUNK):
        per_section(lambda: tok_copy(late, i).start(), lambda: tok_copy(early, i).start())
    for i in range(N_CHUNK):
        wq_copy(i).start()

    def cols(index):
        return pl.ds(pl.multiple_of(index * BLOCK, BLOCK), BLOCK)

    def quarter(index, zz):
        return pl.ds(pl.multiple_of(index * BLOCK + zz * TILE, TILE), TILE)

    def stage_copy(source, o):
        return pltpu.make_async_copy(
            source.at[:, quarter(d_of[o], z)], tok_stage.at[o - 2], stage_sem.at[0, o - 2]
        )

    def cot_stage_copy(o):
        return pltpu.make_async_copy(
            cot.at[:, quarter(d_of[o], y)], cot_stage.at[o - 2], stage_sem.at[1, o - 2]
        )

    def load_rest():
        for i in range(N_CHUNK):
            wo_copy(i).start()

        @pl.when(is_later)
        def _():
            for yy in range(4):
                for zz in range(4):
                    cot_copy(yy, zz).start()

        @pl.when(is_earlier)
        def _():
            for o in (2, 3):
                cot_stage_copy(o).start()

        for o in (2, 3):
            per_section(lambda: stage_copy(early, o).start(), lambda: stage_copy(late, o).start())

    barrier = pltpu.get_barrier_semaphore()
    greeted = z_peer[1:] + y_peer[1:] + [hand_peer]
    greeted += dp_peer[1:] + cross_peer[2:]
    for peer in greeted:
        pl.semaphore_signal(barrier, inc=1, device_id=peer, device_id_type=MESH)

    count = [0]

    def slot():
        count[0] += 1
        return count[0] - 1

    def remote(src, dst, n, peer):
        return pltpu.make_async_remote_copy(
            src_ref=src, dst_ref=dst, send_sem=send_sem.at[n], recv_sem=recv_sem.at[n],
            device_id=peer, device_id_type=MESH,
        )

    xkv[...] = jnp.zeros_like(xkv)
    inv_ref[...] = jnp.zeros_like(inv_ref)

    def scaled(span):
        return (tok[:, span].astype(F32) * gain[0:1, span].astype(F32)).astype(BF16)

    def project_kv(i, carry):
        span = pl.ds(pl.multiple_of(i * CHUNK, CHUNK), CHUNK)
        tok_copy(late, i).wait()
        t = tok[:, span].astype(F32)
        inv_ref[...] += jnp.sum(t * t, axis=1, keepdims=True)
        xkv[...] += dot_nt(scaled(span), wkv[:, span])
        return carry

    wk_copy.wait()
    wv_copy.wait()
    lax.fori_loop(0, N_CHUNK, project_kv, 0, unroll=2)
    inv_ref[...] = lax.rsqrt(inv_ref[...] * (1.0 / D) + 1e-5)
    inv = inv_ref[:, 0:1]

    kv_all[z] = jnp.transpose(xkv[...] * inv).astype(BF16)
    pl.semaphore_wait(barrier, len(greeted))
    kv_slots = [None] + [slot() for _ in range(3)]
    kv_copies = [remote(kv_all.at[z], kv_all.at[z], kv_slots[o], z_peer[o]) for o in (1, 2, 3)]
    for copy in kv_copies:
        copy.start()

    tok_slots = [None] + [slot() for _ in range(3)]
    up_slots = [None] + [slot() for _ in range(3)]
    cot_slots = [None, None, slot(), slot()]
    share_slots = [[slot() for _ in range(3)] for _ in range(2)]
    tok_share_slots = [[slot() for _ in range(3)] for _ in range(2)]

    def tok_send():
        return remote(tok.at[:, cols(d_of[1])], tok_g.at[d], tok_slots[1], dp_peer[1])

    def tok_quarter(o):
        return remote(tok_stage.at[o - 2], tok_part.at[o - 2], tok_slots[o], cross_peer[o])

    def tok_share(o, p):
        return remote(
            tok_part.at[o - 2], tok_g.at[d_of[o], :, quarter(0, z)], tok_share_slots[o - 2][p - 1], z_peer[p]
        )

    def tok_own(o):
        return pltpu.make_async_copy(
            tok_part.at[o - 2], tok_g.at[d_of[o], :, quarter(0, z)], loc_sem.at[o + 4]
        )

    def share_tok():
        for o in (2, 3):
            tok_quarter(o).wait_recv()
            for p in (1, 2, 3):
                tok_share(o, p).start()
            tok_own(o).start()

    def tok_keep():
        return pltpu.make_async_copy(tok.at[:, cols(d)], tok_g.at[d], loc_sem.at[0])

    def up_send(o, zz):
        return remote(up.at[d_of[o], zz], up_g.at[d, :, quarter(0, zz)], up_slots[o], dp_peer[o])

    def up_keep(zz):
        return pltpu.make_async_copy(up.at[d, zz], up_g.at[d, :, quarter(0, zz)], loc_sem.at[1])

    def whole_block(o):
        return remote(tok.at[:, pl.ds(0, BLOCK)], up_g.at[d], up_slots[o], dp_peer[o])

    def whole_keep():
        return pltpu.make_async_copy(tok.at[:, pl.ds(0, BLOCK)], up_g.at[d], loc_sem.at[1])

    def cot_quarter(o):
        return remote(cot_stage.at[o - 2], cot_part.at[o - 2], cot_slots[o], cross_peer[o])

    def cot_share(o, p):
        return remote(
            cot_part.at[o - 2], up_g.at[d_of[o], :, quarter(0, y)], share_slots[o - 2][p - 1], y_peer[p]
        )

    def cot_keep(o):
        return pltpu.make_async_copy(
            cot_part.at[o - 2], up_g.at[d_of[o], :, quarter(0, y)], loc_sem.at[o + 2]
        )

    def send_operands():
        @pl.when(is_earlier)
        def _():
            for o in (2, 3):
                cot_stage_copy(o).wait()
                cot_quarter(o).start()

        for o in (2, 3):
            stage_copy(early, o).wait()
            tok_quarter(o).start()
        tok_send().start()
        tok_keep().start()

    load_rest()
    sent = list(kv_copies)
    received = []

    def finish():
        for copy in sent:
            copy.wait_send()
        for copy in received:
            copy.wait()

        @pl.when(is_later)
        def _():
            for o in (2, 3):
                for p in (1, 2, 3):
                    cot_share(o, p).wait()
                cot_keep(o).wait()
                whole_block(o).wait_send()

        @pl.when(is_earlier)
        def _():
            for o in (2, 3):
                cot_quarter(o).wait_send()
                whole_block(o).wait_recv()
                for k in range(2):
                    for zz in range(4):
                        hop_in(o, k, 0, zz).wait_send()
            for n, index in gathered:
                ref = up.at[0, 0, pl.ds(0, n), :]
                remote(ref, ref, index, hand_peer).wait_send()

        whole_block(1).wait()
        whole_keep().wait()
        tok_send().wait()
        tok_keep().wait()
        for o in (2, 3):
            tok_quarter(o).wait_send()
            for p in (1, 2, 3):
                tok_share(o, p).wait()
            tok_own(o).wait()

    hop_slots = [None, None] + [[[slot() for _ in range(4)][0] for _ in range(2)] for _ in range(2)]

    def hop_in(o, k, yy, zz):
        return remote(
            up.at[yy, zz, pl.ds(k * 128, 128), :], hop.at[o - 2, k, zz], hop_slots[o][k] + zz,
            hand_peer if k == 0 else cross_peer[o],
        )

    def hop_on(o, k, zz):
        return remote(
            hop.at[o - 2, k, zz], up_g.at[d if k == 0 else d_of[o], pl.ds(k * 128, 128), quarter(0, zz)],
            up_slots[o], cross_peer[o] if k == 0 else hand_peer,
        )

    lane = lax.broadcasted_iota(jnp.int32, (SEQ, HD), 1)
    place = lax.broadcasted_iota(jnp.int32, (SEQ, HD), 0)
    offset = (place - begin_of(lens, place)).astype(F32)
    angle = offset * freq[0:1, :]
    cosv[...] = jnp.cos(angle)
    sinv[...] = jnp.where(lane < 64, -1.0, 1.0) * jnp.sin(angle)

    xq[...] = jnp.zeros_like(xq)

    def project_q(i, carry):
        span = pl.ds(pl.multiple_of(i * CHUNK, CHUNK), CHUNK)
        wq_copy(i).wait()
        xq[...] += dot_nn(scaled(span), wq[span, :])
        return carry

    lax.fori_loop(0, N_CHUNK, project_q, 0, unroll=2)
    cos = cosv[...]
    sin = sinv[...]
    cos_t = jnp.transpose(cos)
    sin_t = jnp.transpose(sin)
    for j in range(2):
        q = xq[:, j * HD:(j + 1) * HD] * inv
        q = q * cos + pltpu.roll(q, 64, 1) * sin
        qs[j] = q.astype(BF16)
        qs_t[j] = jnp.transpose(q).astype(BF16)
    inv_t = jnp.transpose(inv_ref[...])[0:1, :]
    for copy in kv_copies:
        copy.wait_recv()
    k = jnp.concatenate([kv_all[i, 0:32] for i in range(4)], axis=0).astype(F32)
    k_t = (k * cos_t + swap_rows(k) * sin_t).astype(BF16)
    v_t = jnp.concatenate([kv_all[i, 32:64] for i in range(4)], axis=0)

    row = lax.broadcasted_iota(jnp.int32, (SEQ, SEQ), 0)
    col = lax.broadcasted_iota(jnp.int32, (SEQ, SEQ), 1)
    allowed = (begin_of(lens, row) == begin_of(lens, col)) & (col <= row)
    for j in range(2):
        scores = jnp.where(allowed, dot_nn(qs[j], k_t) * SCALE, -1e30)
        peak = jnp.max(scores, axis=1, keepdims=True)
        ex = jnp.exp(scores - peak)
        pr = ex / jnp.sum(ex, axis=1, keepdims=True)
        probs[j] = pr
        ctx[j * HD:(j + 1) * HD, :] = dot_nt(v_t, pr.astype(BF16)).astype(BF16)
    ctx_slots = [None] + [slot() for _ in range(3)]
    ctx_copies = [remote(ctx, c_g.at[d], ctx_slots[o], dp_peer[o]) for o in (1, 2, 3)]
    ctx_keep = pltpu.make_async_copy(ctx, c_g.at[d], loc_sem.at[2])
    for copy in ctx_copies:
        copy.start()
    ctx_keep.start()
    received += ctx_copies + [ctx_keep]
    send_operands()

    for i in range(N_CHUNK):
        wo_copy(i).wait()
    dctx[...] = jnp.zeros_like(dctx)

    def wo_rows(yy, zz):
        return pl.ds(pl.multiple_of((yy * 4 + zz) * TILE, TILE), TILE)

    def halves(k):
        return pl.ds(k * 128, 128)

    def offer(k, yy, zz):
        for o in (2, 3):
            @pl.when(yy == d_of[o])
            def _():
                hop_in(o, k, yy, zz).start()

    def add_context(k, yy, zz):
        dctx[halves(k), :] += dot_nn(up[yy, zz, halves(k), :], wo[wo_rows(yy, zz), :])

    own_slots = [slot() for _ in range(2)]
    p1_slots = [[slot() for _ in range(4)] for _ in range(2)]
    p2_slots = [[[slot() for _ in range(4)] for _ in range(4)] for _ in range(2)]

    def hand_copy(g):
        return remote(gin.at[halves(g), :], up.at[y, z, halves(g), :], own_slots[g], hand_peer)

    def at(k, first, second):
        return (second, first) if k == 0 else (first, second)

    @pl.when(is_later)
    def _():
        def body(yy, carry):
            total = dctx[...]
            for zz in range(4):
                cot_copy(yy, zz).wait()
            for zz in range(4):
                total += dot_nn(up[yy, zz], wo[wo_rows(yy, zz), :])
            dctx[...] = total
            return carry

        lax.fori_loop(0, 4, body, 0)

    gathered = []

    @pl.when(is_earlier)
    def _():
        share_tok()
        first_of, second_of = (z, y), (y, z)
        first_right, first_left = (z_right, y_right), (z_left, y_left)
        second_right, second_left = (y_right, z_right), (y_left, z_left)

        def piece(k, a, b, lo, n):
            yy, zz = at(k, a, b)
            return up.at[yy, zz, pl.ds(k * 128 + lo, n), :]

        def send(k, a, b, lo, n, index, peer):
            ref = piece(k, a, b, lo, n)
            remote(ref, ref, index, peer).start()
            gathered.append((n, index))

        def arrived(k, a, b, lo, n, index):
            ref = piece(k, a, b, lo, n)
            remote(ref, ref, index, hand_peer).wait_recv()

        def spread(k, o):
            a = ring(first_of[k] + o)
            send(k, a, second_of[k], 0, 128, p2_slots[k][o][0], second_right[k])
            send(k, a, second_of[k], 0, 128, p2_slots[k][o][1], second_left[k])

        for k in range(2):
            hand_copy(k).wait_recv()
            send(k, first_of[k], second_of[k], 0, 128, p1_slots[k][0], first_right[k])
            send(k, first_of[k], second_of[k], 0, 128, p1_slots[k][1], first_left[k])
            spread(k, 0)
        for k in range(2):
            offer(k, y, z)
            add_context(k, y, z)
        for k in range(2):
            a, b = ring(first_of[k] - 1), second_of[k]
            arrived(k, a, b, 0, 128, p1_slots[k][0])
            send(k, a, b, 0, 64, p1_slots[k][2], first_right[k])
            spread(k, 3)
            a = ring(first_of[k] + 1)
            arrived(k, a, b, 0, 128, p1_slots[k][1])
            send(k, a, b, 64, 64, p1_slots[k][3], first_left[k])
            spread(k, 1)
        for k in range(2):
            for o in (3, 1):
                offer(k, *at(k, ring(first_of[k] + o), second_of[k]))
                add_context(k, *at(k, ring(first_of[k] + o), second_of[k]))

        def relay(k, o):
            a = ring(first_of[k] + o)
            left, right = ring(second_of[k] - 1), ring(second_of[k] + 1)
            arrived(k, a, left, 0, 128, p2_slots[k][o][0])
            send(k, a, left, 0, 64, p2_slots[k][o][2], second_right[k])
            arrived(k, a, right, 0, 128, p2_slots[k][o][1])
            send(k, a, right, 64, 64, p2_slots[k][o][3], second_left[k])
            for b in (left, right):
                offer(k, *at(k, a, b))
                add_context(k, *at(k, a, b))

        for k in range(2):
            relay(k, 0)
        for k in range(2):
            a, b = ring(first_of[k] + 2), second_of[k]
            arrived(k, a, b, 0, 64, p1_slots[k][2])
            arrived(k, a, b, 64, 64, p1_slots[k][3])
            spread(k, 2)
            offer(k, *at(k, a, b))
            add_context(k, *at(k, a, b))
        for o in (3, 1, 2):
            for k in range(2):
                relay(k, o)
        for o in (0, 3, 1, 2):
            for k in range(2):
                a, b = ring(first_of[k] + o), ring(second_of[k] + 2)
                arrived(k, a, b, 0, 64, p2_slots[k][o][2])
                arrived(k, a, b, 64, 64, p2_slots[k][o][3])
                offer(k, *at(k, a, b))
                add_context(k, *at(k, a, b))

    for zz in range(4):
        up_send(1, zz).start()
        up_keep(zz).start()

    dk_t = jnp.zeros((HD, SEQ), F32)
    dv_t = jnp.zeros((HD, SEQ), F32)
    for j in range(2):
        grad = dctx[:, j * HD:(j + 1) * HD]
        pr = probs[j]
        dp = dot_nn(grad.astype(BF16), v_t)
        dss[j] = (pr * (dp - jnp.sum(dp * pr, axis=1, keepdims=True)) * SCALE).astype(BF16)
        dk_t += dot_nn(qs_t[j], dss[j])
        dv_t += dot_nn(jnp.transpose(grad).astype(BF16), pr.astype(BF16))
    dk_t = dk_t * cos_t - swap_rows(dk_t) * sin_t
    for i in range(4):
        kvp_send[i, 0:32] = dk_t[i * 32:(i + 1) * 32].astype(BF16)
        kvp_send[i, 32:64] = dv_t[i * 32:(i + 1) * 32].astype(BF16)
    kvp_slots = [None] + [slot() for _ in range(3)]
    kvp_copies = [
        remote(kvp_send.at[ring(z + o)], kvp_recv.at[o], kvp_slots[o], z_peer[o]) for o in (1, 2, 3)
    ]
    for copy in kvp_copies:
        copy.start()
    sent += kvp_copies
    dq_list = []
    for j in range(2):
        dq = dot_nt(k_t, dss[j])
        dq_list.append(dq * cos_t - swap_rows(dq) * sin_t)
    dq_t = jnp.concatenate(dq_list, axis=0)
    dqkv[0:256, :] = (dq_t * inv_t).astype(BF16)
    dq = jnp.transpose(dq_t)
    aq[...] = (dq * inv).astype(BF16)
    stat = jnp.sum(dq * xq[...], axis=1, keepdims=True)
    for copy in kvp_copies:
        copy.wait_recv()
    dkv_t = kvp_send[z].astype(F32)
    for o in (1, 2, 3):
        dkv_t += kvp_recv[o].astype(F32)
    dqkv[256:320, :] = (dkv_t * inv_t).astype(BF16)
    dkv = jnp.transpose(dkv_t)
    akv[...] = (dkv * inv).astype(BF16)
    stat += jnp.sum(dkv * xkv[...], axis=1, keepdims=True)
    cs_ref[...] = jnp.broadcast_to(inv * inv * inv * stat * (1.0 / D), cs_ref.shape)
    d_slots = [None] + [slot() for _ in range(3)]
    d_copies = [remote(dqkv, d_g.at[d], d_slots[o], dp_peer[o]) for o in (1, 2, 3)]
    d_keep = pltpu.make_async_copy(dqkv, d_g.at[d], loc_sem.at[3])
    for copy in d_copies:
        copy.start()
    d_keep.start()
    received += d_copies + [d_keep]

    ring_of, other_of = (y, z), (z, y)
    right_1, left_1 = (y_right, z_right), (y_left, z_left)
    right_2, left_2 = (z_right, y_right), (z_left, y_left)

    def block(g, a, lo, n):
        if g == 0:
            return part.at[a, pl.ds(lo, n), halves(g), :]
        return part.at[pl.ds(lo, n), a, halves(g), :]

    def tile(k, a, b):
        return (a, b) if k == 0 else (b, a)

    def compute(*tiles):
        for dy, dz in tiles:
            yy, zz = ring(y + dy), ring(z + dz)
            span = wo_rows(yy, zz)
            total = dot_nt(aq[...], wq[span, :]) + dot_nn(akv[...], wkv[:, span])
            total = total * gain[0:1, span].astype(F32) - tok[:, span].astype(F32) * cs_ref[:, 0:1]
            part[yy, zz] = total.astype(BF16)

    rs1 = [[slot() for _ in range(6)] for _ in range(2)]
    rs2 = [[slot() for _ in range(6)] for _ in range(2)]

    def go(src, dst, n, peer):
        copy = remote(src, dst, n, peer)
        copy.start()
        sent.append(copy)

    def landed(ref, n):
        remote(ref, ref, n, y_right).wait_recv()

    def relay_1(g):
        k, i = g, ring_of[g]
        go(block(g, ring(i + 2), 0, 2), rrel.at[g, 0:2], rs1[g][0], right_1[k])
        go(block(g, ring(i + 2), 2, 2), rrel.at[g, 2:4], rs1[g][1], left_1[k])

    def direct_right_1(g):
        k, i = g, ring_of[g]
        go(block(g, ring(i + 1), 2, 2), rdir.at[g, 2:4], rs1[g][5], right_1[k])

    def direct_left_1(g):
        k, i = g, ring_of[g]
        go(block(g, ring(i - 1), 0, 2), rdir.at[g, 0:2], rs1[g][4], left_1[k])

    def add_relay(g, a, b):
        yy, zz = tile(g, a, b)
        part[yy, zz, halves(g), :] = (
            part[yy, zz, halves(g), :].astype(F32) + rrel[g, b].astype(F32)
        ).astype(BF16)

    def accumulate_1(g):
        k, i = g, ring_of[g]
        landed(rrel.at[g, 0:2], rs1[g][0])
        for b in range(2):
            add_relay(g, ring(i + 1), b)
        go(block(g, ring(i + 1), 0, 2), racc.at[g, 0:2], rs1[g][2], right_1[k])
        landed(rrel.at[g, 2:4], rs1[g][1])
        for b in range(2, 4):
            add_relay(g, ring(i - 1), b)
        go(block(g, ring(i - 1), 2, 2), racc.at[g, 2:4], rs1[g][3], left_1[k])

    def collect(g, b):
        yy, zz = tile(g, ring_of[g], b)
        summed[g, b] = (
            part[yy, zz, halves(g), :].astype(F32) + racc[g, b].astype(F32) + rdir[g, b].astype(F32)
        ).astype(BF16)

    def turn(g):
        k, j = g, other_of[g]
        landed(rdir.at[g, 0:2], rs1[g][4])
        landed(rdir.at[g, 2:4], rs1[g][5])
        landed(racc.at[g, 0:2], rs1[g][2])
        landed(racc.at[g, 2:4], rs1[g][3])
        collect(g, ring(j + 2))
        go(summed.at[g, ring(j + 2), 0:64], rrel2.at[g, 0:64], rs2[g][0], right_2[k])
        go(summed.at[g, ring(j + 2), 64:128], rrel2.at[g, 64:128], rs2[g][1], left_2[k])
        collect(g, ring(j + 1))
        go(summed.at[g, ring(j + 1), 64:128], rdir2.at[g, 64:128], rs2[g][5], right_2[k])
        collect(g, ring(j - 1))
        go(summed.at[g, ring(j - 1), 0:64], rdir2.at[g, 0:64], rs2[g][4], left_2[k])
        collect(g, j)

    def accumulate_2(g):
        k, j = g, other_of[g]
        landed(rrel2.at[g, 0:64], rs2[g][0])
        a = ring(j + 1)
        summed[g, a, 0:64] = (summed[g, a, 0:64].astype(F32) + rrel2[g, 0:64].astype(F32)).astype(BF16)
        go(summed.at[g, a, 0:64], racc2.at[g, 0:64], rs2[g][2], right_2[k])
        landed(rrel2.at[g, 64:128], rs2[g][1])
        a = ring(j - 1)
        summed[g, a, 64:128] = (summed[g, a, 64:128].astype(F32) + rrel2[g, 64:128].astype(F32)).astype(BF16)
        go(summed.at[g, a, 64:128], racc2.at[g, 64:128], rs2[g][3], left_2[k])

    def result(g):
        j = other_of[g]
        landed(rdir2.at[g, 0:64], rs2[g][4])
        landed(rdir2.at[g, 64:128], rs2[g][5])
        landed(racc2.at[g, 0:64], rs2[g][2])
        landed(racc2.at[g, 64:128], rs2[g][3])
        gin[halves(g), :] = (
            up[y, z, halves(g), :].astype(F32)
            + summed[g, j].astype(F32)
            + racc2[g].astype(F32)
            + rdir2[g].astype(F32)
        ).astype(BF16)
        pl.when(is_later)(lambda: hand_copy(g).start())

    compute((2, 2), (2, 1), (2, 3), (2, 0))
    relay_1(0)
    compute((1, 2), (3, 2), (0, 2))
    relay_1(1)
    compute((1, 1), (1, 3), (1, 0))
    direct_right_1(0)
    compute((3, 1), (3, 3), (3, 0))
    direct_left_1(0)
    compute((0, 1), (0, 3))
    direct_right_1(1)
    direct_left_1(1)
    compute((0, 0))
    for step in (accumulate_1, turn, accumulate_2, result):
        step(0)
        step(1)

    @pl.when(is_later)
    def _():
        share_tok()
        for o in (2, 3):
            cot_quarter(o).wait_recv()
            for p in (1, 2, 3):
                cot_share(o, p).start()
            cot_keep(o).start()
        for dz in (0, 3, 1, 2):
            for k in range(2):
                for o in (2, 3):
                    zz = ring(z + dz)
                    hop_in(o, k, 0, zz).wait_recv()
                    hop_on(o, k, zz).start()
        for g in range(2):
            hand_copy(g).wait_send()

    finish()


N_SLOTS = 6 + 3 + 2 + 12 + 16 + 3 + 2 + 8 + 32 + 3 + 3 + 24


def relay(late, cot, early, lens, gain, w_q, w_k, w_v, w_o, freq):
    any_spec = pl.BlockSpec(memory_space=pl.ANY)
    vmem = pl.BlockSpec(memory_space=pltpu.VMEM)
    smem = pl.BlockSpec(memory_space=pltpu.SMEM)
    out_shape = (
        jax.ShapeDtypeStruct((SEQ, TILE), BF16),
        jax.ShapeDtypeStruct((4, SEQ, BLOCK), BF16),
        jax.ShapeDtypeStruct((4, SEQ, BLOCK), BF16),
        jax.ShapeDtypeStruct((4, ROWS, SEQ), BF16),
        jax.ShapeDtypeStruct((4, SEQ, SEQ), BF16),
    )
    scratch = [
        pltpu.VMEM((SEQ, D), BF16),
        pltpu.VMEM((D, 256), BF16),
        pltpu.VMEM((KV, D), BF16),
        pltpu.VMEM((D, 256), BF16),
        pltpu.VMEM((4, 4, SEQ, TILE), BF16),
        pltpu.VMEM((4, 4, SEQ, TILE), BF16),
        pltpu.VMEM((SEQ, 256), F32),
        pltpu.VMEM((SEQ, KV), F32),
        pltpu.VMEM((SEQ, 256), F32),
        pltpu.VMEM((2, SEQ, SEQ), F32),
        pltpu.VMEM((2, SEQ, SEQ), BF16),
        pltpu.VMEM((2, SEQ, HD), BF16),
        pltpu.VMEM((2, HD, SEQ), BF16),
        pltpu.VMEM((4, KV, SEQ), BF16),
        pltpu.VMEM((4, KV, SEQ), BF16),
        pltpu.VMEM((4, KV, SEQ), BF16),
        pltpu.VMEM((SEQ, HD), F32),
        pltpu.VMEM((SEQ, HD), F32),
        pltpu.VMEM((SEQ, HD), F32),
        pltpu.VMEM((SEQ, HD), F32),
        pltpu.VMEM((SEQ, 256), BF16),
        pltpu.VMEM((SEQ, KV), BF16),
        pltpu.VMEM((ROWS, SEQ), BF16),
        pltpu.VMEM((256, SEQ), BF16),
        pltpu.VMEM((2, 4, 128, TILE), BF16),
        pltpu.VMEM((2, 4, 128, TILE), BF16),
        pltpu.VMEM((2, 4, 128, TILE), BF16),
        pltpu.VMEM((2, 4, 128, TILE), BF16),
        pltpu.VMEM((2, 128, TILE), BF16),
        pltpu.VMEM((2, 128, TILE), BF16),
        pltpu.VMEM((2, 128, TILE), BF16),
        pltpu.VMEM((2, 2, 4, 128, TILE), BF16),
        pltpu.VMEM((2, SEQ, TILE), BF16),
        pltpu.VMEM((2, SEQ, TILE), BF16),
        pltpu.VMEM((2, SEQ, TILE), BF16),
        pltpu.VMEM((2, SEQ, TILE), BF16),
        pltpu.SemaphoreType.DMA((5, N_CHUNK)),
        pltpu.SemaphoreType.DMA((4, 4)),
        pltpu.SemaphoreType.DMA((2, 2)),
        pltpu.SemaphoreType.DMA((8,)),
        pltpu.SemaphoreType.DMA((N_SLOTS,)),
        pltpu.SemaphoreType.DMA((N_SLOTS,)),
    ]
    return pl.pallas_call(
        relay_kernel,
        out_shape=out_shape,
        in_specs=[any_spec, any_spec, any_spec, smem, vmem, any_spec, any_spec, any_spec, any_spec, vmem],
        out_specs=(vmem, any_spec, any_spec, any_spec, any_spec),
        scratch_shapes=scratch,
        compiler_params=pltpu.CompilerParams(
            collective_id=0, has_side_effects=True, vmem_limit_bytes=62 * 1024 * 1024
        ),
        name="relay",
    )(late, cot, early, lens, gain, w_q, w_k, w_v, w_o, freq)


def weights_kernel(tok, up, d_ref, c_ref, gain, gin, q_out, o_out, k_out, v_out, gin_out):
    i = pl.program_id(0)
    start = pl.multiple_of(lax.axis_index("dp") * BLOCK + i * TILE, TILE)
    total = dot_nn(d_ref[0], tok[0])
    for e in range(1, 4):
        total += dot_nn(d_ref[e], tok[e])
    total = total * gain[0:1, pl.ds(start, TILE)].astype(F32)
    q_out[...] = jnp.transpose(total[0:256]).astype(BF16)
    k_out[...] = total[256:288].astype(BF16)
    v_out[...] = total[288:320].astype(BF16)
    other = dot_nn(c_ref[0], up[0])
    for e in range(1, 4):
        other += dot_nn(c_ref[e], up[e])
    o_out[...] = jnp.transpose(other).astype(BF16)
    gin_out[...] = gin[...]


def weight_grads(tok_g, up_g, d_g, c_g, gain, gin):
    return pl.pallas_call(
        weights_kernel,
        grid=(4,),
        out_shape=(
            jax.ShapeDtypeStruct((BLOCK, 256), BF16),
            jax.ShapeDtypeStruct((BLOCK, 256), BF16),
            jax.ShapeDtypeStruct((32, BLOCK), BF16),
            jax.ShapeDtypeStruct((32, BLOCK), BF16),
            jax.ShapeDtypeStruct((SEQ, TILE), BF16),
        ),
        in_specs=[
            pl.BlockSpec((4, SEQ, TILE), lambda i: (0, 0, i)),
            pl.BlockSpec((4, SEQ, TILE), lambda i: (0, 0, i)),
            pl.BlockSpec((4, ROWS, SEQ), lambda i: (0, 0, 0)),
            pl.BlockSpec((4, SEQ, SEQ), lambda i: (0, 0, 0)),
            pl.BlockSpec((1, D), lambda i: (0, 0)),
            pl.BlockSpec((SEQ, TILE), lambda i: (0, 0)),
        ],
        out_specs=(
            pl.BlockSpec((TILE, 256), lambda i: (i, 0)),
            pl.BlockSpec((TILE, 256), lambda i: (i, 0)),
            pl.BlockSpec((32, TILE), lambda i: (0, i)),
            pl.BlockSpec((32, TILE), lambda i: (0, i)),
            pl.BlockSpec((SEQ, TILE), lambda i: (0, 0)),
        ),
        compiler_params=pltpu.CompilerParams(vmem_limit_bytes=62 * 1024 * 1024),
        name="weight_grads",
    )(tok_g, up_g, d_g, c_g, gain, gin)


def on_device(
    late_inputs, cotangent, early_inputs, doc_lengths, norm_gain, w_query, w_key, w_value, w_output
):
    half = 10000.0 ** (-np.arange(0, HD, 2).astype(np.float32) / HD)
    freq = jnp.asarray(np.concatenate([half, half]).astype(np.float32)[None, :])
    gin, tok_g, up_g, d_g, c_g = relay(
        late_inputs, cotangent, early_inputs, doc_lengths, norm_gain,
        w_query[0], w_key[0].T, w_value[0].T, w_output[0], freq,
    )
    grad_q, grad_o, grad_k, grad_v, grad_in = weight_grads(tok_g, up_g, d_g, c_g, norm_gain, gin)
    return grad_in[None], grad_q[None], grad_k.T[None], grad_v.T[None], grad_o[None]


def solution(mesh):
    in_specs = (
        P("dp", None),
        P("dp", None),
        P("dp", None),
        P("dp", None),
        P("section", None),
        P("section", None, "mp"),
        P("section", None, "mp"),
        P("section", None, "mp"),
        P("section", None, "mp"),
    )
    out_specs = (P("section", "dp", "mp"),) * 5
    return jax.shard_map(
        on_device, mesh=mesh, in_specs=in_specs, out_specs=out_specs, check_vma=False
    )
```

```python
import functools
import math

import jax
import jax.numpy as jnp
import numpy as np
from jax import lax
from jax.experimental import pallas as pl
from jax.experimental.pallas import tpu as pltpu
from jax.sharding import PartitionSpec as P

HD = 128
SEQ = 256
D = 8192
TILE = 512
BLOCK = 2048
KV = 64
STEP = 1024
ROWS = 320
CHUNK = 1024
N_CHUNK = D // CHUNK
FIRST_TILES = [(2, 2), (2, 1), (2, 3), (2, 0), (1, 2), (3, 2), (0, 2)]
SCALE = 1.0 / math.sqrt(HD)
F32 = jnp.float32
BF16 = jnp.bfloat16
MESH = pl.DeviceIdType.MESH


def dot_nn(a, b):
    return lax.dot_general(a, b, (((1,), (0,)), ((), ())), preferred_element_type=F32)


def dot_nt(a, b):
    return lax.dot_general(a, b, (((1,), (1,)), ((), ())), preferred_element_type=F32)


def ring(v):
    return lax.rem(v + 4, 4)


def begin_of(lens, places):
    start = jnp.int32(0)
    begins = jnp.zeros_like(places)
    for i in range(4):
        begins = jnp.maximum(begins, jnp.where(places >= start, start, 0))
        start = start + lens[0, i]
    return begins


def swap_rows(v):
    return jnp.concatenate([v[64:128], v[0:64]], axis=0)


def relay_kernel(
    late, cot, early, lens, gain, w_q, w_k, w_v, w_o, freq,
    gin, tok_g, up_g, d_g, c_g,
    tok, wq, wkv, wo, up, part,
    xq, xkv, dctx, probs, dss, qs, qs_t, kv_all, kvp_send, kvp_recv, cosv, sinv, inv_ref, cs_ref,
    aq, akv, dqkv, ctx, early_sum,
    rrel, racc, rdir, summed, rrel2, racc2, rdir2, hop, tok_stage, tok_part, cot_stage, cot_part,
    load_sem, up_sem, stage_sem, loc_sem, send_sem, recv_sem,
):
    s = lax.axis_index("section")
    d = lax.axis_index("dp")
    m = lax.axis_index("mp")
    y, z = lax.div(m, 4), lax.rem(m, 4)
    h, c = lax.div(d, 2), lax.rem(d, 2)
    d_of = [d, h * 2 + (1 - c), (1 - h) * 2 + c, (1 - h) * 2 + (1 - c)]
    is_later = s == 1
    is_earlier = s == 0

    def mp_id(yy, zz):
        return {"mp": yy * 4 + zz}

    z_peer = [mp_id(y, ring(z + o)) for o in range(4)]
    y_peer = [mp_id(ring(y + o), z) for o in range(4)]
    y_right, y_left = y_peer[1], y_peer[3]
    z_right, z_left = z_peer[1], z_peer[3]
    dp_peer = [{"dp": d_of[o]} for o in range(4)]
    cross_peer = [None, None] + [{"section": 1 - s, "dp": d_of[o]} for o in (2, 3)]
    hand_peer = {"section": 1 - s}

    def tok_copy(source, i):
        return pltpu.make_async_copy(
            source.at[:, pl.ds(i * CHUNK, CHUNK)], tok.at[:, pl.ds(i * CHUNK, CHUNK)], load_sem.at[0, i]
        )

    def wq_copy(i):
        return pltpu.make_async_copy(
            w_q.at[pl.ds(i * CHUNK, CHUNK), :], wq.at[pl.ds(i * CHUNK, CHUNK), :], load_sem.at[1, i]
        )

    wk_copy = pltpu.make_async_copy(w_k, wkv.at[0:32, :], load_sem.at[2, 0])
    wv_copy = pltpu.make_async_copy(w_v, wkv.at[32:64, :], load_sem.at[3, 0])

    def wo_copy(i):
        return pltpu.make_async_copy(
            w_o.at[pl.ds(i * CHUNK, CHUNK), :], wo.at[pl.ds(i * CHUNK, CHUNK), :], load_sem.at[4, i]
        )

    def cot_copy(yy, zz):
        return pltpu.make_async_copy(
            cot.at[:, pl.ds(pl.multiple_of((yy * 4 + zz) * TILE, TILE), TILE)], up.at[yy, zz], up_sem.at[yy, zz]
        )

    def per_section(later, earlier):
        pl.when(is_later)(later)
        pl.when(is_earlier)(earlier)

    wk_copy.start()
    wv_copy.start()
    for i in range(N_CHUNK):
        per_section(lambda: tok_copy(late, i).start(), lambda: tok_copy(early, i).start())
    for i in range(N_CHUNK):
        wq_copy(i).start()

    def cols(index):
        return pl.ds(pl.multiple_of(index * BLOCK, BLOCK), BLOCK)

    def quarter(index, zz):
        return pl.ds(pl.multiple_of(index * BLOCK + zz * TILE, TILE), TILE)

    def stage_copy(source, o):
        return pltpu.make_async_copy(
            source.at[:, quarter(d_of[o], z)], tok_stage.at[o - 2], stage_sem.at[0, o - 2]
        )

    def cot_stage_copy(o):
        return pltpu.make_async_copy(
            cot.at[:, quarter(d_of[o], y)], cot_stage.at[o - 2], stage_sem.at[1, o - 2]
        )

    def load_rest():
        for i in range(N_CHUNK):
            wo_copy(i).start()

        @pl.when(is_later)
        def _():
            for yy in range(4):
                for zz in range(4):
                    cot_copy(yy, zz).start()

        @pl.when(is_earlier)
        def _():
            for o in (2, 3):
                cot_stage_copy(o).start()

        for o in (2, 3):
            per_section(lambda: stage_copy(early, o).start(), lambda: stage_copy(late, o).start())

    barrier = pltpu.get_barrier_semaphore()
    greeted = z_peer[1:] + y_peer[1:] + [hand_peer]
    greeted += dp_peer[1:] + cross_peer[2:]
    for peer in greeted:
        pl.semaphore_signal(barrier, inc=1, device_id=peer, device_id_type=MESH)

    count = [0]

    def slot():
        count[0] += 1
        return count[0] - 1

    def remote(src, dst, n, peer):
        return pltpu.make_async_remote_copy(
            src_ref=src, dst_ref=dst, send_sem=send_sem.at[n], recv_sem=recv_sem.at[n],
            device_id=peer, device_id_type=MESH,
        )

    xkv[...] = jnp.zeros_like(xkv)
    inv_ref[...] = jnp.zeros_like(inv_ref)

    def scaled(span):
        return (tok[:, span].astype(F32) * gain[0:1, span].astype(F32)).astype(BF16)

    def project_kv(i, carry):
        span = pl.ds(pl.multiple_of(i * CHUNK, CHUNK), CHUNK)
        tok_copy(late, i).wait()
        t = tok[:, span].astype(F32)
        inv_ref[...] += jnp.sum(t * t, axis=1, keepdims=True)
        xkv[...] += dot_nt(scaled(span), wkv[:, span])
        return carry

    wk_copy.wait()
    wv_copy.wait()
    lax.fori_loop(0, N_CHUNK, project_kv, 0, unroll=2)
    inv_ref[...] = lax.rsqrt(inv_ref[...] * (1.0 / D) + 1e-5)
    inv = inv_ref[:, 0:1]

    kv_all[z] = jnp.transpose(xkv[...] * inv).astype(BF16)
    pl.semaphore_wait(barrier, len(greeted))
    kv_slots = [None] + [slot() for _ in range(3)]
    kv_copies = [remote(kv_all.at[z], kv_all.at[z], kv_slots[o], z_peer[o]) for o in (1, 2, 3)]
    for copy in kv_copies:
        copy.start()

    tok_slots = [None] + [slot() for _ in range(3)]
    up_slots = [None] + [slot() for _ in range(3)]
    cot_slots = [None, None, slot(), slot()]
    share_slots = [[slot() for _ in range(3)] for _ in range(2)]
    tok_share_slots = [[slot() for _ in range(3)] for _ in range(2)]

    def tok_send():
        return remote(tok.at[:, cols(d_of[1])], tok_g.at[d], tok_slots[1], dp_peer[1])

    def tok_quarter(o):
        return remote(tok_stage.at[o - 2], tok_part.at[o - 2], tok_slots[o], cross_peer[o])

    def tok_share(o, p):
        return remote(
            tok_part.at[o - 2], tok_g.at[d_of[o], :, quarter(0, z)], tok_share_slots[o - 2][p - 1], z_peer[p]
        )

    def tok_own(o):
        return pltpu.make_async_copy(
            tok_part.at[o - 2], tok_g.at[d_of[o], :, quarter(0, z)], loc_sem.at[o + 4]
        )

    def share_tok():
        for o in (2, 3):
            tok_quarter(o).wait_recv()
            for p in (1, 2, 3):
                tok_share(o, p).start()
            tok_own(o).start()

    def tok_keep():
        return pltpu.make_async_copy(tok.at[:, cols(d)], tok_g.at[d], loc_sem.at[0])

    def up_send(o, zz):
        return remote(up.at[d_of[o], zz], up_g.at[d, :, quarter(0, zz)], up_slots[o], dp_peer[o])

    def up_keep(zz):
        return pltpu.make_async_copy(up.at[d, zz], up_g.at[d, :, quarter(0, zz)], loc_sem.at[1])

    def whole_block(o):
        return remote(tok.at[:, pl.ds(0, BLOCK)], up_g.at[d], up_slots[o], dp_peer[o])

    def whole_keep():
        return pltpu.make_async_copy(tok.at[:, pl.ds(0, BLOCK)], up_g.at[d], loc_sem.at[1])

    def cot_quarter(o):
        return remote(cot_stage.at[o - 2], cot_part.at[o - 2], cot_slots[o], cross_peer[o])

    def cot_share(o, p):
        return remote(
            cot_part.at[o - 2], up_g.at[d_of[o], :, quarter(0, y)], share_slots[o - 2][p - 1], y_peer[p]
        )

    def cot_keep(o):
        return pltpu.make_async_copy(
            cot_part.at[o - 2], up_g.at[d_of[o], :, quarter(0, y)], loc_sem.at[o + 2]
        )

    def send_operands():
        @pl.when(is_earlier)
        def _():
            for o in (2, 3):
                cot_stage_copy(o).wait()
                cot_quarter(o).start()

        for o in (2, 3):
            stage_copy(early, o).wait()
            tok_quarter(o).start()
        tok_send().start()
        tok_keep().start()

    load_rest()
    sent = list(kv_copies)
    received = []

    def finish():
        for copy in sent:
            copy.wait_send()
        for copy in received:
            copy.wait()

        @pl.when(is_later)
        def _():
            for o in (2, 3):
                for p in (1, 2, 3):
                    cot_share(o, p).wait()
                cot_keep(o).wait()
                whole_block(o).wait_send()

        @pl.when(is_earlier)
        def _():
            for o in (2, 3):
                cot_quarter(o).wait_send()
                whole_block(o).wait_recv()
                for k in range(2):
                    for zz in range(4):
                        hop_in(o, k, 0, zz).wait_send()
            for n, index in gathered:
                ref = up.at[0, 0, pl.ds(0, n), :]
                remote(ref, ref, index, hand_peer).wait_send()

        whole_block(1).wait()
        whole_keep().wait()
        tok_send().wait()
        tok_keep().wait()
        for o in (2, 3):
            tok_quarter(o).wait_send()
            for p in (1, 2, 3):
                tok_share(o, p).wait()
            tok_own(o).wait()

    hop_slots = [None, None] + [[[slot() for _ in range(4)][0] for _ in range(2)] for _ in range(2)]

    def hop_in(o, k, yy, zz):
        return remote(
            up.at[yy, zz, pl.ds(k * 128, 128), :], hop.at[o - 2, k, zz], hop_slots[o][k] + zz,
            hand_peer if k == 0 else cross_peer[o],
        )

    def hop_on(o, k, zz):
        return remote(
            hop.at[o - 2, k, zz], up_g.at[d if k == 0 else d_of[o], pl.ds(k * 128, 128), quarter(0, zz)],
            up_slots[o], cross_peer[o] if k == 0 else hand_peer,
        )

    lane = lax.broadcasted_iota(jnp.int32, (SEQ, HD), 1)
    place = lax.broadcasted_iota(jnp.int32, (SEQ, HD), 0)
    offset = (place - begin_of(lens, place)).astype(F32)
    angle = offset * freq[0:1, :]
    cosv[...] = jnp.cos(angle)
    sinv[...] = jnp.where(lane < 64, -1.0, 1.0) * jnp.sin(angle)

    xq[...] = jnp.zeros_like(xq)

    def project_q(i, carry):
        span = pl.ds(pl.multiple_of(i * CHUNK, CHUNK), CHUNK)
        wq_copy(i).wait()
        xq[...] += dot_nn(scaled(span), wq[span, :])
        return carry

    lax.fori_loop(0, N_CHUNK, project_q, 0, unroll=2)
    cos = cosv[...]
    sin = sinv[...]
    cos_t = jnp.transpose(cos)
    sin_t = jnp.transpose(sin)
    for j in range(2):
        q = xq[:, j * HD:(j + 1) * HD] * inv
        q = q * cos + pltpu.roll(q, 64, 1) * sin
        qs[j] = q.astype(BF16)
        qs_t[j] = jnp.transpose(q).astype(BF16)
    inv_t = jnp.transpose(inv_ref[...])[0:1, :]
    for i in range(N_CHUNK):
        wo_copy(i).wait()
    dctx[...] = jnp.zeros_like(dctx)

    def wo_rows(yy, zz):
        return pl.ds(pl.multiple_of((yy * 4 + zz) * TILE, TILE), TILE)

    @pl.when(is_later)
    def _():
        def body(yy, carry):
            total = dctx[...]
            for zz in range(4):
                cot_copy(yy, zz).wait()
            for zz in range(4):
                total += dot_nn(up[yy, zz], wo[wo_rows(yy, zz), :])
            dctx[...] = total
            return carry

        lax.fori_loop(0, 4, body, 0)

    for copy in kv_copies:
        copy.wait_recv()
    k = jnp.concatenate([kv_all[i, 0:32] for i in range(4)], axis=0).astype(F32)
    k_t = (k * cos_t + swap_rows(k) * sin_t).astype(BF16)
    v_t = jnp.concatenate([kv_all[i, 32:64] for i in range(4)], axis=0)

    row = lax.broadcasted_iota(jnp.int32, (SEQ, SEQ), 0)
    col = lax.broadcasted_iota(jnp.int32, (SEQ, SEQ), 1)
    allowed = (begin_of(lens, row) == begin_of(lens, col)) & (col <= row)
    for j in range(2):
        scores = jnp.where(allowed, dot_nn(qs[j], k_t) * SCALE, -1e30)
        peak = jnp.max(scores, axis=1, keepdims=True)
        ex = jnp.exp(scores - peak)
        pr = ex / jnp.sum(ex, axis=1, keepdims=True)
        probs[j] = pr
        ctx[j * HD:(j + 1) * HD, :] = dot_nt(v_t, pr.astype(BF16)).astype(BF16)
    own_cols = pl.ds(pl.multiple_of(d * SEQ, SEQ), SEQ)
    ctx_slots = [None] + [slot() for _ in range(3)]
    ctx_copies = [remote(ctx, c_g.at[:, own_cols], ctx_slots[o], dp_peer[o]) for o in (1, 2, 3)]
    ctx_keep = pltpu.make_async_copy(ctx, c_g.at[:, own_cols], loc_sem.at[2])
    for copy in ctx_copies:
        copy.start()
    ctx_keep.start()
    received += ctx_copies + [ctx_keep]
    send_operands()

    def halves(k):
        return pl.ds(k * 128, 128)

    def offer(k, yy, zz):
        for o in (2, 3):
            @pl.when(yy == d_of[o])
            def _():
                hop_in(o, k, yy, zz).start()

    def add_context(k, yy, zz):
        dctx[halves(k), :] += dot_nn(up[yy, zz, halves(k), :], wo[wo_rows(yy, zz), :])

    own_slots = [slot() for _ in range(2)]
    p1_slots = [[slot() for _ in range(4)] for _ in range(2)]
    p2_slots = [[[slot() for _ in range(4)] for _ in range(4)] for _ in range(2)]

    def hand_copy(g):
        return remote(gin.at[halves(g), :], up.at[y, z, halves(g), :], own_slots[g], hand_peer)

    def at(k, first, second):
        return (second, first) if k == 0 else (first, second)

    gathered = []

    @pl.when(is_earlier)
    def _():
        share_tok()
        first_of, second_of = (z, y), (y, z)
        first_right, first_left = (z_right, y_right), (z_left, y_left)
        second_right, second_left = (y_right, z_right), (y_left, z_left)

        def piece(k, a, b, lo, n):
            yy, zz = at(k, a, b)
            return up.at[yy, zz, pl.ds(k * 128 + lo, n), :]

        def send(k, a, b, lo, n, index, peer):
            ref = piece(k, a, b, lo, n)
            remote(ref, ref, index, peer).start()
            gathered.append((n, index))

        def arrived(k, a, b, lo, n, index):
            ref = piece(k, a, b, lo, n)
            remote(ref, ref, index, hand_peer).wait_recv()

        def spread(k, o):
            a = ring(first_of[k] + o)
            send(k, a, second_of[k], 0, 128, p2_slots[k][o][0], second_right[k])
            send(k, a, second_of[k], 0, 128, p2_slots[k][o][1], second_left[k])

        for k in range(2):
            hand_copy(k).wait_recv()
            send(k, first_of[k], second_of[k], 0, 128, p1_slots[k][0], first_right[k])
            send(k, first_of[k], second_of[k], 0, 128, p1_slots[k][1], first_left[k])
            spread(k, 0)
        for k in range(2):
            offer(k, y, z)
            add_context(k, y, z)
        for k in range(2):
            a, b = ring(first_of[k] - 1), second_of[k]
            arrived(k, a, b, 0, 128, p1_slots[k][0])
            send(k, a, b, 0, 64, p1_slots[k][2], first_right[k])
            spread(k, 3)
            a = ring(first_of[k] + 1)
            arrived(k, a, b, 0, 128, p1_slots[k][1])
            send(k, a, b, 64, 64, p1_slots[k][3], first_left[k])
            spread(k, 1)
        for k in range(2):
            for o in (3, 1):
                offer(k, *at(k, ring(first_of[k] + o), second_of[k]))
                add_context(k, *at(k, ring(first_of[k] + o), second_of[k]))

        def relay(k, o):
            a = ring(first_of[k] + o)
            left, right = ring(second_of[k] - 1), ring(second_of[k] + 1)
            arrived(k, a, left, 0, 128, p2_slots[k][o][0])
            send(k, a, left, 0, 64, p2_slots[k][o][2], second_right[k])
            arrived(k, a, right, 0, 128, p2_slots[k][o][1])
            send(k, a, right, 64, 64, p2_slots[k][o][3], second_left[k])
            for b in (left, right):
                offer(k, *at(k, a, b))
                add_context(k, *at(k, a, b))

        for k in range(2):
            relay(k, 0)
        for k in range(2):
            a, b = ring(first_of[k] + 2), second_of[k]
            arrived(k, a, b, 0, 64, p1_slots[k][2])
            arrived(k, a, b, 64, 64, p1_slots[k][3])
            spread(k, 2)
            offer(k, *at(k, a, b))
            add_context(k, *at(k, a, b))
        for o in (3, 1, 2):
            for k in range(2):
                relay(k, o)
        for o in (0, 3, 1, 2):
            for k in range(2):
                a, b = ring(first_of[k] + o), ring(second_of[k] + 2)
                arrived(k, a, b, 0, 64, p2_slots[k][o][2])
                arrived(k, a, b, 64, 64, p2_slots[k][o][3])
                offer(k, *at(k, a, b))
                add_context(k, *at(k, a, b))

    for zz in range(4):
        up_send(1, zz).start()
        up_keep(zz).start()

    dk_t = jnp.zeros((HD, SEQ), F32)
    dv_t = jnp.zeros((HD, SEQ), F32)
    for j in range(2):
        grad = dctx[:, j * HD:(j + 1) * HD]
        pr = probs[j]
        dp = dot_nn(grad.astype(BF16), v_t)
        dss[j] = (pr * (dp - jnp.sum(dp * pr, axis=1, keepdims=True)) * SCALE).astype(BF16)
        dk_t += dot_nn(qs_t[j], dss[j])
        dv_t += dot_nn(jnp.transpose(grad).astype(BF16), pr.astype(BF16))
    dk_t = dk_t * cos_t - swap_rows(dk_t) * sin_t
    for i in range(4):
        kvp_send[i, 0:32] = dk_t[i * 32:(i + 1) * 32].astype(BF16)
        kvp_send[i, 32:64] = dv_t[i * 32:(i + 1) * 32].astype(BF16)
    kvp_slots = [None] + [slot() for _ in range(3)]
    kvp_copies = [
        remote(kvp_send.at[ring(z + o)], kvp_recv.at[o], kvp_slots[o], z_peer[o]) for o in (1, 2, 3)
    ]
    for copy in kvp_copies:
        copy.start()
    sent += kvp_copies
    dq_list = []
    for j in range(2):
        dq = dot_nt(k_t, dss[j])
        dq_list.append(dq * cos_t - swap_rows(dq) * sin_t)
    dq_t = jnp.concatenate(dq_list, axis=0)
    dqkv[0:256, :] = (dq_t * inv_t).astype(BF16)
    dq = jnp.transpose(dq_t)
    aq[...] = (dq * inv).astype(BF16)
    stat = jnp.sum(dq * xq[...], axis=1, keepdims=True)
    for n, (dy, dz) in enumerate(FIRST_TILES):
        early_sum[n] = dot_nt(aq[...], wq[wo_rows(ring(y + dy), ring(z + dz)), :])
    for copy in kvp_copies:
        copy.wait_recv()
    dkv_t = kvp_send[z].astype(F32)
    for o in (1, 2, 3):
        dkv_t += kvp_recv[o].astype(F32)
    dqkv[256:320, :] = (dkv_t * inv_t).astype(BF16)
    dkv = jnp.transpose(dkv_t)
    akv[...] = (dkv * inv).astype(BF16)
    stat += jnp.sum(dkv * xkv[...], axis=1, keepdims=True)
    cs_ref[...] = jnp.broadcast_to(inv * inv * inv * stat * (1.0 / D), cs_ref.shape)
    d_slots = [None] + [slot() for _ in range(3)]
    d_copies = [remote(dqkv, d_g.at[:, own_cols], d_slots[o], dp_peer[o]) for o in (1, 2, 3)]
    d_keep = pltpu.make_async_copy(dqkv, d_g.at[:, own_cols], loc_sem.at[3])
    for copy in d_copies:
        copy.start()
    d_keep.start()
    received += d_copies + [d_keep]

    ring_of, other_of = (y, z), (z, y)
    right_1, left_1 = (y_right, z_right), (y_left, z_left)
    right_2, left_2 = (z_right, y_right), (z_left, y_left)

    def block(g, a, lo, n):
        if g == 0:
            return part.at[a, pl.ds(lo, n), halves(g), :]
        return part.at[pl.ds(lo, n), a, halves(g), :]

    def tile(k, a, b):
        return (a, b) if k == 0 else (b, a)

    def compute(*tiles):
        for dy, dz in tiles:
            yy, zz = ring(y + dy), ring(z + dz)
            span = wo_rows(yy, zz)
            total = dot_nn(akv[...], wkv[:, span])
            if (dy, dz) in FIRST_TILES:
                total += early_sum[FIRST_TILES.index((dy, dz))]
            else:
                total += dot_nt(aq[...], wq[span, :])
            total = total * gain[0:1, span].astype(F32) - tok[:, span].astype(F32) * cs_ref[:, 0:1]
            part[yy, zz] = total.astype(BF16)

    rs1 = [[slot() for _ in range(6)] for _ in range(2)]
    rs2 = [[slot() for _ in range(6)] for _ in range(2)]

    def go(src, dst, n, peer):
        copy = remote(src, dst, n, peer)
        copy.start()
        sent.append(copy)

    def landed(ref, n):
        remote(ref, ref, n, y_right).wait_recv()

    def relay_1(g):
        k, i = g, ring_of[g]
        go(block(g, ring(i + 2), 0, 2), rrel.at[g, 0:2], rs1[g][0], right_1[k])
        go(block(g, ring(i + 2), 2, 2), rrel.at[g, 2:4], rs1[g][1], left_1[k])

    def direct_right_1(g):
        k, i = g, ring_of[g]
        go(block(g, ring(i + 1), 2, 2), rdir.at[g, 2:4], rs1[g][5], right_1[k])

    def direct_left_1(g):
        k, i = g, ring_of[g]
        go(block(g, ring(i - 1), 0, 2), rdir.at[g, 0:2], rs1[g][4], left_1[k])

    def add_relay(g, a, b):
        yy, zz = tile(g, a, b)
        part[yy, zz, halves(g), :] = (
            part[yy, zz, halves(g), :].astype(F32) + rrel[g, b].astype(F32)
        ).astype(BF16)

    def accumulate_1(g):
        k, i = g, ring_of[g]
        landed(rrel.at[g, 0:2], rs1[g][0])
        for b in range(2):
            add_relay(g, ring(i + 1), b)
        go(block(g, ring(i + 1), 0, 2), racc.at[g, 0:2], rs1[g][2], right_1[k])
        landed(rrel.at[g, 2:4], rs1[g][1])
        for b in range(2, 4):
            add_relay(g, ring(i - 1), b)
        go(block(g, ring(i - 1), 2, 2), racc.at[g, 2:4], rs1[g][3], left_1[k])

    def collect(g, b):
        yy, zz = tile(g, ring_of[g], b)
        summed[g, b] = (
            part[yy, zz, halves(g), :].astype(F32) + racc[g, b].astype(F32) + rdir[g, b].astype(F32)
        ).astype(BF16)

    def turn(g):
        k, j = g, other_of[g]
        landed(rdir.at[g, 0:2], rs1[g][4])
        landed(rdir.at[g, 2:4], rs1[g][5])
        landed(racc.at[g, 0:2], rs1[g][2])
        landed(racc.at[g, 2:4], rs1[g][3])
        collect(g, ring(j + 2))
        go(summed.at[g, ring(j + 2), 0:64], rrel2.at[g, 0:64], rs2[g][0], right_2[k])
        go(summed.at[g, ring(j + 2), 64:128], rrel2.at[g, 64:128], rs2[g][1], left_2[k])
        collect(g, ring(j + 1))
        go(summed.at[g, ring(j + 1), 64:128], rdir2.at[g, 64:128], rs2[g][5], right_2[k])
        collect(g, ring(j - 1))
        go(summed.at[g, ring(j - 1), 0:64], rdir2.at[g, 0:64], rs2[g][4], left_2[k])
        collect(g, j)

    def accumulate_2(g):
        k, j = g, other_of[g]
        landed(rrel2.at[g, 0:64], rs2[g][0])
        a = ring(j + 1)
        summed[g, a, 0:64] = (summed[g, a, 0:64].astype(F32) + rrel2[g, 0:64].astype(F32)).astype(BF16)
        go(summed.at[g, a, 0:64], racc2.at[g, 0:64], rs2[g][2], right_2[k])
        landed(rrel2.at[g, 64:128], rs2[g][1])
        a = ring(j - 1)
        summed[g, a, 64:128] = (summed[g, a, 64:128].astype(F32) + rrel2[g, 64:128].astype(F32)).astype(BF16)
        go(summed.at[g, a, 64:128], racc2.at[g, 64:128], rs2[g][3], left_2[k])

    def result(g):
        j = other_of[g]
        landed(rdir2.at[g, 0:64], rs2[g][4])
        landed(rdir2.at[g, 64:128], rs2[g][5])
        landed(racc2.at[g, 0:64], rs2[g][2])
        landed(racc2.at[g, 64:128], rs2[g][3])
        gin[halves(g), :] = (
            up[y, z, halves(g), :].astype(F32)
            + summed[g, j].astype(F32)
            + racc2[g].astype(F32)
            + rdir2[g].astype(F32)
        ).astype(BF16)
        pl.when(is_later)(lambda: hand_copy(g).start())

    compute((2, 2), (2, 1), (2, 3), (2, 0))
    relay_1(0)
    compute((1, 2), (3, 2), (0, 2))
    relay_1(1)
    compute((1, 1), (1, 3), (1, 0))
    direct_right_1(0)
    compute((3, 1), (3, 3), (3, 0))
    direct_left_1(0)
    compute((0, 1), (0, 3))
    direct_right_1(1)
    direct_left_1(1)
    compute((0, 0))
    for step in (accumulate_1, turn, accumulate_2, result):
        step(0)
        step(1)

    @pl.when(is_later)
    def _():
        share_tok()
        for o in (2, 3):
            cot_quarter(o).wait_recv()
            for p in (1, 2, 3):
                cot_share(o, p).start()
            cot_keep(o).start()
        for dz in (0, 3, 1, 2):
            for k in range(2):
                for o in (2, 3):
                    zz = ring(z + dz)
                    hop_in(o, k, 0, zz).wait_recv()
                    hop_on(o, k, zz).start()
        for g in range(2):
            hand_copy(g).wait_send()

    finish()


N_SLOTS = 6 + 3 + 2 + 12 + 16 + 3 + 2 + 8 + 32 + 3 + 3 + 24


def relay(late, cot, early, lens, gain, w_q, w_k, w_v, w_o, freq):
    any_spec = pl.BlockSpec(memory_space=pl.ANY)
    vmem = pl.BlockSpec(memory_space=pltpu.VMEM)
    smem = pl.BlockSpec(memory_space=pltpu.SMEM)
    out_shape = (
        jax.ShapeDtypeStruct((SEQ, TILE), BF16),
        jax.ShapeDtypeStruct((4, SEQ, BLOCK), BF16),
        jax.ShapeDtypeStruct((4, SEQ, BLOCK), BF16),
        jax.ShapeDtypeStruct((ROWS, 4 * SEQ), BF16),
        jax.ShapeDtypeStruct((SEQ, 4 * SEQ), BF16),
    )
    scratch = [
        pltpu.VMEM((SEQ, D), BF16),
        pltpu.VMEM((D, 256), BF16),
        pltpu.VMEM((KV, D), BF16),
        pltpu.VMEM((D, 256), BF16),
        pltpu.VMEM((4, 4, SEQ, TILE), BF16),
        pltpu.VMEM((4, 4, SEQ, TILE), BF16),
        pltpu.VMEM((SEQ, 256), F32),
        pltpu.VMEM((SEQ, KV), F32),
        pltpu.VMEM((SEQ, 256), F32),
        pltpu.VMEM((2, SEQ, SEQ), F32),
        pltpu.VMEM((2, SEQ, SEQ), BF16),
        pltpu.VMEM((2, SEQ, HD), BF16),
        pltpu.VMEM((2, HD, SEQ), BF16),
        pltpu.VMEM((4, KV, SEQ), BF16),
        pltpu.VMEM((4, KV, SEQ), BF16),
        pltpu.VMEM((4, KV, SEQ), BF16),
        pltpu.VMEM((SEQ, HD), F32),
        pltpu.VMEM((SEQ, HD), F32),
        pltpu.VMEM((SEQ, HD), F32),
        pltpu.VMEM((SEQ, HD), F32),
        pltpu.VMEM((SEQ, 256), BF16),
        pltpu.VMEM((SEQ, KV), BF16),
        pltpu.VMEM((ROWS, SEQ), BF16),
        pltpu.VMEM((256, SEQ), BF16),
        pltpu.VMEM((len(FIRST_TILES), SEQ, TILE), F32),
        pltpu.VMEM((2, 4, 128, TILE), BF16),
        pltpu.VMEM((2, 4, 128, TILE), BF16),
        pltpu.VMEM((2, 4, 128, TILE), BF16),
        pltpu.VMEM((2, 4, 128, TILE), BF16),
        pltpu.VMEM((2, 128, TILE), BF16),
        pltpu.VMEM((2, 128, TILE), BF16),
        pltpu.VMEM((2, 128, TILE), BF16),
        pltpu.VMEM((2, 2, 4, 128, TILE), BF16),
        pltpu.VMEM((2, SEQ, TILE), BF16),
        pltpu.VMEM((2, SEQ, TILE), BF16),
        pltpu.VMEM((2, SEQ, TILE), BF16),
        pltpu.VMEM((2, SEQ, TILE), BF16),
        pltpu.SemaphoreType.DMA((5, N_CHUNK)),
        pltpu.SemaphoreType.DMA((4, 4)),
        pltpu.SemaphoreType.DMA((2, 2)),
        pltpu.SemaphoreType.DMA((8,)),
        pltpu.SemaphoreType.DMA((N_SLOTS,)),
        pltpu.SemaphoreType.DMA((N_SLOTS,)),
    ]
    return pl.pallas_call(
        relay_kernel,
        out_shape=out_shape,
        in_specs=[any_spec, any_spec, any_spec, smem, vmem, any_spec, any_spec, any_spec, any_spec, vmem],
        out_specs=(vmem, any_spec, any_spec, any_spec, any_spec),
        scratch_shapes=scratch,
        compiler_params=pltpu.CompilerParams(
            collective_id=0, has_side_effects=True, vmem_limit_bytes=62 * 1024 * 1024
        ),
        name="relay",
    )(late, cot, early, lens, gain, w_q, w_k, w_v, w_o, freq)


def weights_kernel(tok, up, d_ref, c_ref, gain, gin, q_out, o_out, k_out, v_out, gin_out):
    i = pl.program_id(0)
    start = pl.multiple_of(lax.axis_index("dp") * BLOCK + i * STEP, STEP)
    total = dot_nn(d_ref[...], tok[...].reshape(4 * SEQ, STEP))
    total = total * gain[0:1, pl.ds(start, STEP)].astype(F32)
    q_out[...] = jnp.transpose(total[0:256]).astype(BF16)
    k_out[...] = total[256:288].astype(BF16)
    v_out[...] = total[288:320].astype(BF16)
    other = dot_nn(c_ref[...], up[...].reshape(4 * SEQ, STEP))
    o_out[...] = jnp.transpose(other).astype(BF16)
    gin_out[...] = gin[...]


def weight_grads(tok_g, up_g, d_g, c_g, gain, gin):
    return pl.pallas_call(
        weights_kernel,
        grid=(BLOCK // STEP,),
        out_shape=(
            jax.ShapeDtypeStruct((BLOCK, 256), BF16),
            jax.ShapeDtypeStruct((BLOCK, 256), BF16),
            jax.ShapeDtypeStruct((32, BLOCK), BF16),
            jax.ShapeDtypeStruct((32, BLOCK), BF16),
            jax.ShapeDtypeStruct((SEQ, TILE), BF16),
        ),
        in_specs=[
            pl.BlockSpec((4, SEQ, STEP), lambda i: (0, 0, i)),
            pl.BlockSpec((4, SEQ, STEP), lambda i: (0, 0, i)),
            pl.BlockSpec((ROWS, 4 * SEQ), lambda i: (0, 0)),
            pl.BlockSpec((SEQ, 4 * SEQ), lambda i: (0, 0)),
            pl.BlockSpec((1, D), lambda i: (0, 0)),
            pl.BlockSpec((SEQ, TILE), lambda i: (0, 0)),
        ],
        out_specs=(
            pl.BlockSpec((STEP, 256), lambda i: (i, 0)),
            pl.BlockSpec((STEP, 256), lambda i: (i, 0)),
            pl.BlockSpec((32, STEP), lambda i: (0, i)),
            pl.BlockSpec((32, STEP), lambda i: (0, i)),
            pl.BlockSpec((SEQ, TILE), lambda i: (0, 0)),
        ),
        compiler_params=pltpu.CompilerParams(vmem_limit_bytes=62 * 1024 * 1024),
        name="weight_grads",
    )(tok_g, up_g, d_g, c_g, gain, gin)


def on_device(
    late_inputs, cotangent, early_inputs, doc_lengths, norm_gain, w_query, w_key, w_value, w_output
):
    half = 10000.0 ** (-np.arange(0, HD, 2).astype(np.float32) / HD)
    freq = jnp.asarray(np.concatenate([half, half]).astype(np.float32)[None, :])
    gin, tok_g, up_g, d_g, c_g = relay(
        late_inputs, cotangent, early_inputs, doc_lengths, norm_gain,
        w_query[0], w_key[0].T, w_value[0].T, w_output[0], freq,
    )
    grad_q, grad_o, grad_k, grad_v, grad_in = weight_grads(tok_g, up_g, d_g, c_g, norm_gain, gin)
    return grad_in[None], grad_q[None], grad_k.T[None], grad_v.T[None], grad_o[None]


def solution(mesh):
    in_specs = (
        P("dp", None),
        P("dp", None),
        P("dp", None),
        P("dp", None),
        P("section", None),
        P("section", None, "mp"),
        P("section", None, "mp"),
        P("section", None, "mp"),
        P("section", None, "mp"),
    )
    out_specs = (P("section", "dp", "mp"),) * 5
    return jax.shard_map(
        on_device, mesh=mesh, in_specs=in_specs, out_specs=out_specs, check_vma=False
    )
```
